256 devices in a mesh: gx: 8 (over y, x_lo), gy: 32 (over z, x_hi, core).
Axes of the slice: x: 4 (x_hi: 2, x_lo: 2; x = x_hi * 2 + x_lo), y: 4, z: 8, core: 2. Of those that a mesh axis runs over, the one named last changes fastest.
Arguments:
- old_fields: float32 [4, 256, 512, 128], P(None, 'gx', 'gy'), may hold values from -12 to 12, as said below
- inverse_step: float32 [256, 512, 128], P('gx', 'gy'), may hold values from 8 to 64
- boundary: int32 [256, 512, 128], P('gx', 'gy'), may hold values from 0 to 1, as said below
Outputs:
- new_fields: float32 [4, 256, 512, 128], P(None, 'gx', 'gy')
- pressure: float32 [256, 512, 128], P('gx', 'gy')
The draws below stay inside these ranges and needn't reach their ends.
Inputs may be any that keep to these rules, and one draw needn't show every extreme that they name: `old_fields`: drawn with a random sign and a magnitude that may vary over the brick. `boundary`: all copies of one mesh node hold the same value; the lowest node layer of every column and the top node plane are 0, and a column may have up to three fixed bottom layers.
All inputs are finite; a program needn't handle non-finite values.
Results may differ from the reference program's by a relative error of at most 0.00012.
Values sent between devices are 32-bit elements; how exact they have to be, the bound alone decides.
A program may use at most 64 MiB of HBM per device.

```python
import math
import jax
import jax.numpy as jnp
import numpy as np
from jax import lax

EZ = 16
ITERS = 6
CHEB = 6
NXP = 256
NYP = 512
NZP = 128


def draw_old_fields(key, part):
    key = jax.random.fold_in(key, 5)
    envelope = 1.0 + (jnp.arange(NXP, dtype=jnp.float32) / NXP).reshape(1, NXP, 1, 1) + (jnp.arange(NYP, dtype=jnp.float32) / NYP).reshape(1, 1, NYP, 1)
    sample = jnp.clip(jax.random.normal(key, (4, NXP, NYP, NZP), jnp.float32), -4.0, 4.0)
    return sample * envelope


def draw_boundary(key, part):
    key = jax.random.fold_in(key, 11)
    columns_x = NXP // 8 * 7
    columns_y = NYP // 8 * 7
    heights = jax.random.randint(key, (columns_x, columns_y), 1, 4)
    place_x = (jnp.arange(NXP) // 8 * 7 + jnp.arange(NXP) % 8) % columns_x
    place_y = (jnp.arange(NYP) // 8 * 7 + jnp.arange(NYP) % 8) % columns_y
    level_index = jnp.arange(NZP) // 8 * 7 + jnp.arange(NZP) % 8
    ground = heights[place_x[:, None], place_y[None, :]]
    pinned = (level_index[None, None, :] < ground[:, :, None]) | (level_index[None, None, :] == EZ * 7)
    return jnp.where(pinned, 0, 1).astype(jnp.int32)


def steps_of(stream_key, extent, shards, low, top_value):
    level = 1.0
    for dim, parts in shards:
        steps = jax.random.uniform(jax.random.fold_in(jax.random.fold_in(stream_key, 6), dim), (parts,), jnp.float32, low / len(shards), top_value / len(shards))
        level = level * jnp.repeat(jnp.exp(steps), extent[dim] // parts).reshape((-1,) + (1,) * (len(extent) - 1 - dim))
    return level


def setup_inputs(seed: int = 0) -> dict:
    arg_keys = jax.random.split(jax.random.key(seed), 4)
    return {
        "old_fields": draw_old_fields(jax.random.fold_in(arg_keys[3], 71), 0),
        "inverse_step": jnp.clip(jnp.exp(math.log(64.0) - 2.0794415 * jax.random.uniform(arg_keys[1], (NXP, NYP, NZP), jnp.float32) ** steps_of(arg_keys[1], (NXP, NYP, NZP), ((0, 8), (1, 32)), -0.2, 0.2)), 8.0, 64.0),
        "boundary": draw_boundary(jax.random.fold_in(arg_keys[3], 71), 0),
    }


SIGMA_SHIFT = 0.5
DIFFUSE = (1.0, 1.0, 1.0, 1.4)
COUPLING = 1.0
STRATIFY = 1.0
SPREAD = 20.0
HIGHEST_PRECISION = lax.Precision.HIGHEST
LOBATTO_POINTS = (-1.0, -0.8717401485096066, -0.5917001814331423, -0.2092992179024789, 0.2092992179024789, 0.5917001814331423, 0.8717401485096066, 1.0)


def legendre_value(points, degree):
    previous = points * 0.0 + 1.0
    current = points
    for order in range(1, degree):
        following = ((2 * order + 1) * points * current - order * previous) / (order + 1)
        previous = current
        current = following
    return current


def quadrature_tables():
    degree = 7
    points = np.array(LOBATTO_POINTS)
    values = legendre_value(points, degree)
    weights = 2.0 / (degree * (degree + 1) * values * values)
    derive = np.zeros((degree + 1, degree + 1))
    for row_index in range(degree + 1):
        for column_index in range(degree + 1):
            if row_index != column_index:
                derive[row_index, column_index] = values[row_index] / (values[column_index] * (points[row_index] - points[column_index]))
    derive[0, 0] = -degree * (degree + 1) / 4.0
    derive[degree, degree] = degree * (degree + 1) / 4.0
    stiffness_table = derive.T @ (weights[:, None] * derive)
    return weights, derive, stiffness_table


def node_lines(vector, extent_x, extent_y, extent_z):
    line_x = jnp.asarray(np.tile(vector, extent_x // 8), jnp.float32).reshape(extent_x, 1, 1)
    line_y = jnp.asarray(np.tile(vector, extent_y // 8), jnp.float32).reshape(extent_y, 1)
    line_z = jnp.asarray(np.tile(vector, extent_z // 8), jnp.float32)
    return line_x, line_y, line_z


def along_first(nodal, matrix):
    components, extent_x, extent_y, extent_z = nodal.shape
    blocks = nodal.reshape(components, extent_x // 8, 8, extent_y, extent_z)
    contracted = jnp.einsum("ab,pebyz->peayz", jnp.asarray(matrix, jnp.float32), blocks, precision=HIGHEST_PRECISION)
    return contracted.reshape(nodal.shape)


def along_second(nodal, matrix):
    components, extent_x, extent_y, extent_z = nodal.shape
    blocks = nodal.reshape(components, extent_x, extent_y // 8, 8, extent_z)
    contracted = jnp.einsum("ab,pxebz->pxeaz", jnp.asarray(matrix, jnp.float32), blocks, precision=HIGHEST_PRECISION)
    return contracted.reshape(nodal.shape)


def along_third(nodal, matrix):
    components, extent_x, extent_y, extent_z = nodal.shape
    blocks = nodal.reshape(components, extent_x, extent_y, extent_z // 8, 8)
    contracted = jnp.einsum("ab,pxyeb->pxyea", jnp.asarray(matrix, jnp.float32), blocks, precision=HIGHEST_PRECISION)
    return contracted.reshape(nodal.shape)


def stiffness(nodal):
    weights, derive, stiffness_table = quadrature_tables()
    weight_x, weight_y, weight_z = node_lines(weights, nodal.shape[1], nodal.shape[2], nodal.shape[3])
    total = along_first(nodal, stiffness_table) * weight_y * weight_z
    total = total + along_second(nodal, stiffness_table) * weight_x * weight_z
    return total + along_third(nodal, stiffness_table) * weight_x * weight_y


def pair_sum(nodal, dimension, preceding, following):
    length = nodal.shape[dimension]
    before = jnp.concatenate([preceding, lax.slice_in_dim(nodal, 0, length - 1, axis=dimension)], axis=dimension)
    after_plane = jnp.concatenate([lax.slice_in_dim(nodal, 1, length, axis=dimension), following], axis=dimension)
    layout = [1] * nodal.ndim
    layout[dimension] = length
    position = (jnp.arange(length) % 8).reshape(layout)
    return nodal + jnp.where(position == 0, before, 0.0) + jnp.where(position == 7, after_plane, 0.0)


def assemble(nodal):
    nodal = pair_sum(nodal, 1, nodal[:, -1:], nodal[:, :1])
    nodal = pair_sum(nodal, 2, nodal[:, :, -1:], nodal[:, :, :1])
    empty_plane = jnp.zeros_like(nodal[:, :, :, :1])
    return pair_sum(nodal, 3, empty_plane, empty_plane)


def multiplicity_weights(extent_x, extent_y, extent_z):
    along_x = jnp.where(jnp.arange(extent_x) % 8 % 7 == 0, 0.5, 1.0).astype(jnp.float32)
    along_y = jnp.where(jnp.arange(extent_y) % 8 % 7 == 0, 0.5, 1.0).astype(jnp.float32)
    index_z = jnp.arange(extent_z)
    shared_z = (index_z % 8 % 7 == 0) & (index_z > 0) & (index_z < extent_z - 1)
    along_z = jnp.where(shared_z, 0.5, 1.0).astype(jnp.float32)
    return along_x.reshape(extent_x, 1, 1) * along_y.reshape(extent_y, 1) * along_z


def products(left_field, right_field, multiplicity):
    return jnp.sum(left_field * right_field * multiplicity, axis=(1, 2, 3))


def chebyshev_bounds():
    weights, derive, stiffness_table = quadrature_tables()
    weight_matrix = np.eye(8) * weights
    element_matrix = np.kron(np.kron(stiffness_table, weight_matrix), weight_matrix)
    element_matrix = element_matrix + np.kron(np.kron(weight_matrix, stiffness_table), weight_matrix)
    element_matrix = element_matrix + np.kron(np.kron(weight_matrix, weight_matrix), stiffness_table)
    element_matrix = element_matrix + SIGMA_SHIFT * np.kron(np.kron(weight_matrix, weight_matrix), weight_matrix)
    diagonal_index = np.arange(element_matrix.shape[0])
    bounds_ratio = np.sum(np.abs(element_matrix), axis=1) / element_matrix[diagonal_index, diagonal_index]
    upper_bound = float(np.max(bounds_ratio))
    lower_bound = upper_bound / SPREAD
    return (upper_bound + lower_bound) / 2.0, (upper_bound - lower_bound) / 2.0


def reference(old_fields, inverse_step, boundary):
    weights, derive, stiffness_table = quadrature_tables()
    free_nodes = boundary.astype(jnp.float32)
    extent_x, extent_y, extent_z = inverse_step.shape
    weight_x, weight_y, weight_z = node_lines(weights, extent_x, extent_y, extent_z)
    mass_weights = weight_x * weight_y * weight_z
    multiplicity = multiplicity_weights(extent_x, extent_y, extent_z)
    diffuse = jnp.asarray(np.array(DIFFUSE), jnp.float32).reshape(4, 1, 1, 1)
    nothing = jnp.zeros_like(old_fields[0])
    buoyancy = jnp.stack([nothing, nothing, COUPLING * old_fields[3], -STRATIFY * old_fields[2]])
    residual = free_nodes * assemble(mass_weights * (inverse_step * old_fields + buoyancy))
    solution = jnp.zeros_like(old_fields)
    direction = residual
    norm_now = products(residual, residual, multiplicity)
    for iteration in range(ITERS):
        applied = free_nodes * assemble(diffuse * stiffness(direction) + inverse_step * mass_weights * direction)
        step_size = (norm_now / products(direction, applied, multiplicity)).reshape(4, 1, 1, 1)
        solution = solution + step_size * direction
        residual = residual - step_size * applied
        norm_next = products(residual, residual, multiplicity)
        direction = residual + (norm_next / norm_now).reshape(4, 1, 1, 1) * direction
        norm_now = norm_next
    spread = along_first(solution[0:1], derive) + along_second(solution[1:2], derive) + along_third(solution[2:3], derive)
    source_term = -free_nodes * assemble(mass_weights * spread)
    table_index = np.arange(8)
    diag_x, diag_y, diag_z = node_lines(stiffness_table[table_index, table_index], extent_x, extent_y, extent_z)
    local_diagonal = diag_x * weight_y * weight_z + weight_x * diag_y * weight_z + weight_x * weight_y * diag_z + SIGMA_SHIFT * mass_weights
    diagonal = assemble(local_diagonal[None])
    inverse = 1.0 / diagonal
    centre_value, half_width = chebyshev_bounds()
    factor = centre_value / half_width
    pressure = jnp.zeros_like(source_term)
    remainder = source_term
    update = inverse * remainder / centre_value
    damping = 1.0 / factor
    for iteration in range(CHEB):
        pressure = pressure + update
        if iteration < CHEB - 1:
            remainder = remainder - free_nodes * assemble(stiffness(update) + SIGMA_SHIFT * mass_weights * update)
            damping_next = 1.0 / (2.0 * factor - damping)
            update = damping_next * damping * update + (2.0 * damping_next / half_width) * inverse * remainder
            damping = damping_next
    return solution, pressure[0]
```

```python
import jax
import jax.numpy as jnp
import ml_dtypes
import numpy as np
from jax import lax
from jax.experimental import pallas as pl
from jax.experimental.pallas import tpu as pltpu
from jax.sharding import PartitionSpec as P

ITERS = 6
CHEB = 6
SIGMA_SHIFT = 0.5
THERMAL = 1.4
COUPLING = 1.0
STRATIFY = 1.0
SPREAD = 20.0
CENTRE = 6.0
HALF = 2.9
LOBATTO_POINTS = (
    -1.0,
    -0.8717401485096066,
    -0.5917001814331423,
    -0.2092992179024789,
    0.2092992179024789,
    0.5917001814331423,
    0.8717401485096066,
    1.0,
)
MESH = pl.DeviceIdType.MESH
LX, LY, LZ = 32, 16, 128
ELEMENTS = LX // 8
F32 = jnp.float32
FACES = (
    (-1, 0, 0, 16, 16),
    (1, 0, 16, 0, 16),
    (0, -1, 32, 64, 32),
    (0, 1, 64, 32, 32),
    (-1, -1, 96, 120, 8),
    (-1, 1, 104, 112, 8),
    (1, -1, 112, 104, 8),
    (1, 1, 120, 96, 8),
)


def legendre_value(points, degree):
    previous = points * 0.0 + 1.0
    current = points
    for order in range(1, degree):
        following = ((2 * order + 1) * points * current - order * previous) / (order + 1)
        previous = current
        current = following
    return current


def quadrature_tables():
    degree = 7
    points = np.array(LOBATTO_POINTS)
    values = legendre_value(points, degree)
    weights = 2.0 / (degree * (degree + 1) * values * values)
    derive = np.zeros((degree + 1, degree + 1))
    for row in range(degree + 1):
        for column in range(degree + 1):
            if row != column:
                derive[row, column] = values[row] / (
                    values[column] * (points[row] - points[column])
                )
    derive[0, 0] = -degree * (degree + 1) / 4.0
    derive[degree, degree] = degree * (degree + 1) / 4.0
    return weights, derive, derive.T @ (weights[:, None] * derive)


def chebyshev_bounds():
    weights, _, stiff = quadrature_tables()
    w = np.diag(weights)
    element = np.kron(np.kron(stiff, w), w)
    element = element + np.kron(np.kron(w, stiff), w)
    element = element + np.kron(np.kron(w, w), stiff)
    element = element + SIGMA_SHIFT * np.kron(np.kron(w, w), w)
    upper = float(np.max(np.sum(np.abs(element), axis=1) / np.diag(element)))
    lower = upper / SPREAD
    return (upper + lower) / 2.0, (upper - lower) / 2.0


def chebyshev_coefficients():
    centre, half = chebyshev_bounds()
    ratio = centre / half
    damping = 1.0 / ratio
    pairs = [(0.0, 1.0 / centre)]
    for _ in range(CHEB - 1):
        following = 1.0 / (2.0 * ratio - damping)
        pairs.append((following * damping, 2.0 * following / half))
        damping = following
    return pairs


def split_pair(matrix):
    high = matrix.astype(ml_dtypes.bfloat16)
    low = (matrix - high.astype(np.float64)).astype(ml_dtypes.bfloat16)
    return high, low


def left_table(matrix):
    high, low = split_pair(matrix)
    return np.block([[high, high], [low, np.zeros_like(low)]])


def right_table(matrix):
    high, low = split_pair(matrix)
    return np.block([[high, low], [high, np.zeros_like(low)]])


def matrix_tables():
    weights, derive, stiff = quadrature_tables()
    scaled = stiff / weights[:, None]
    eye_y = np.eye(LY // 8)
    eye_z = np.eye(LZ // 8)
    lap_xy = np.kron(scaled, np.eye(LY)) + np.kron(np.eye(8), np.kron(eye_y, scaled))
    lap_z = np.kron(eye_z, scaled).T
    div_xy = np.concatenate(
        [np.kron(derive, np.eye(LY)), np.kron(np.eye(8), np.kron(eye_y, derive))], axis=1
    )
    div_z = np.kron(eye_z, derive).T
    return np.stack(
        [
            left_table(lap_xy),
            right_table(lap_z),
            np.concatenate(split_pair(div_xy), axis=0),
            right_table(div_z),
        ]
    )


def field_tables():
    weights, _, stiff = quadrature_tables()
    mass = weights[:, None, None] * np.tile(weights, 2)[None, :, None] * np.tile(weights, 16)
    shared = np.where(np.arange(8) % 7 == 0, 0.5, 1.0)
    shared_z = np.tile(shared, 16)
    shared_z[0] = shared_z[-1] = 1.0
    part = shared[:, None, None] * np.tile(shared, 2)[None, :, None] * shared_z

    def periodic(line):
        line = line.copy()
        line[0] = line[7] = line[0] + line[7]
        return line

    def column(line):
        line = np.tile(line, 16)
        total = line.copy()
        total[8::8] += line[7:-1:8]
        total[7:-1:8] += line[8::8]
        return total

    entry = np.diag(stiff)
    wx, sx = periodic(weights), periodic(entry)
    wy, sy = np.tile(wx, 2), np.tile(sx, 2)
    wz, sz = column(weights), column(entry)

    def outer(a, b, c):
        return a[:, None, None] * b[None, :, None] * c

    diagonal = outer(sx, wy, wz) + outer(wx, sy, wz) + outer(wx, wy, sz)
    diagonal = diagonal + SIGMA_SHIFT * outer(wx, wy, wz)
    return np.stack([mass / HALF, part, HALF / diagonal]).astype(np.float32)


def reduction_stages(nx, ny):
    bits_y = ny.bit_length() - 1
    bits = list(range(bits_y + nx.bit_length() - 1))
    stages = [[b for b in bits if b < 2 or b >= bits_y], [b for b in bits if 2 <= b < bits_y]]
    return [stage for stage in stages if stage]


def step_kernel(nx, ny, *refs):
    (old_hbm, inv_hbm, bnd_hbm, mat_ref, tab_ref, new_hbm, prs_hbm) = refs[:7]
    (old, inv, bnd, free, minv, basis, fields, rem, upd, prs) = refs[7:17]
    (vsnd, vrcv, psnd, prcv, macc, arow, arcv) = refs[17:24]
    (lsem, vss, vrs, pss, prs_sem, ass, ars, osem) = refs[24:]

    gx = lax.axis_index("gx")
    gy = lax.axis_index("gy")

    def neighbour(dx, dy):
        return (lax.rem(gx + dx + nx, nx), lax.rem(gy + dy + ny, ny))

    me = gx * ny + gy
    stages = []
    for bits in reduction_stages(nx, ny):
        partners = []
        for mask in range(1, 1 << len(bits)):
            other = me
            for place, b in enumerate(bits):
                if mask >> place & 1:
                    other = other + (1 - 2 * lax.rem(lax.div(me, 1 << b), 2)) * (1 << b)
            partners.append((mask, (lax.div(other, ny), lax.rem(other, ny))))
        stages.append(partners)

    loads = [
        pltpu.make_async_copy(inv_hbm, inv, lsem.at[0]),
        pltpu.make_async_copy(bnd_hbm, bnd, lsem.at[1]),
        pltpu.make_async_copy(old_hbm, old, lsem.at[2]),
    ]
    for load in loads:
        load.start()

    barrier = pltpu.get_barrier_semaphore()
    greeted = 0
    for dx, dy, *_ in FACES:
        pl.semaphore_signal(barrier, inc=1, device_id=neighbour(dx, dy), device_id_type=MESH)
        greeted += 1
    for partners in stages:
        for _, device in partners:
            pl.semaphore_signal(barrier, inc=1, device_id=device, device_id_type=MESH)
            greeted += 1

    lane = lax.broadcasted_iota(jnp.int32, (128, 128), 1)
    z_first = (lax.rem(lane, 8) == 0) & (lane > 0)
    z_last = (lax.rem(lane, 8) == 7) & (lane < LZ - 1)
    row3 = lax.broadcasted_iota(jnp.int32, (8, 8, 128), 1)
    row3_first, row3_last = row3 == 0, row3 == 7
    row = lax.broadcasted_iota(jnp.int32, (8, 128), 0)
    row_first, row_last = row == 0, row == 7
    tile_lane = lax.broadcasted_iota(jnp.int32, (8, 128), 1)

    def planes(e):
        return pl.ds(8 * e, 8)

    def inner_sums(w):
        flat = w.reshape(128, 128)
        flat = (
            flat
            + jnp.where(z_first, pltpu.roll(flat, 1, 1), 0.0)
            + jnp.where(z_last, pltpu.roll(flat, 127, 1), 0.0)
        )
        w = flat.reshape(8, LY, 128)
        a, b = w[:, :8], w[:, 8:]
        a_sum = a + jnp.where(row3_last, pltpu.roll(b, 7, 1), 0.0)
        b_sum = b + jnp.where(row3_first, pltpu.roll(a, 1, 1), 0.0)
        return jnp.concatenate([a_sum, b_sum], axis=1)

    def assembled(local, emit):
        before = None
        for e in range(ELEMENTS):
            w = inner_sums(local(e))
            if before is not None:
                both = before[7:] + w[:1]
                emit(e - 1, jnp.concatenate([before[:7], both], axis=0))
                w = jnp.concatenate([both, w[1:]], axis=0)
            before = w
        emit(ELEMENTS - 1, before)

    def pack(ref, e, w):
        ref[pl.ds(32 + 8 * e, 8), :] = w[:, 0, :]
        ref[pl.ds(64 + 8 * e, 8), :] = w[:, LY - 1, :]
        if e == 0:
            ref[pl.ds(0, 16), :] = w[0]
            ref[pl.ds(96, 1), :] = w[0, :1]
            ref[pl.ds(104, 1), :] = w[0, LY - 1 :]
        if e == ELEMENTS - 1:
            ref[pl.ds(16, 16), :] = w[7]
            ref[pl.ds(112, 1), :] = w[7, :1]
            ref[pl.ds(120, 1), :] = w[7, LY - 1 :]

    def spread_row(ref, r):
        return jnp.broadcast_to(ref[pl.ds(r, 1), :], (8, 128))

    def halo(ref, e):
        out = []
        for x in range(8):
            first = spread_row(ref, 32 + 8 * e + x)
            last = spread_row(ref, 64 + 8 * e + x)
            side = None
            if e == 0 and x == 0:
                side, corner = 0, 96
            if e == ELEMENTS - 1 and x == 7:
                side, corner = 16, 112
            if side is not None:
                first = first + spread_row(ref, corner)
                last = last + spread_row(ref, corner + 8)
            first = jnp.where(row_first, first, 0.0)
            last = jnp.where(row_last, last, 0.0)
            if side is not None:
                first = first + ref[pl.ds(side, 8), :]
                last = last + ref[pl.ds(side + 8, 8), :]
            out.append(jnp.concatenate([first, last], axis=0))
        return jnp.stack(out)

    def send_faces(src, dst, send_sem, recv_sem):
        for dx, dy, here, there, rows in FACES:
            pltpu.make_async_remote_copy(
                src_ref=src.at[pl.ds(here, rows)],
                dst_ref=dst.at[pl.ds(there, rows)],
                send_sem=send_sem,
                recv_sem=recv_sem,
                device_id=neighbour(dx, dy),
                device_id_type=MESH,
            ).start()

    def wait_all(ref, sem):
        pltpu.make_async_copy(ref, ref, sem).wait()

    def halves(v):
        high = v.astype(jnp.bfloat16)
        return high, (v - high.astype(F32)).astype(jnp.bfloat16)

    def along_z(high, low, index):
        out = jnp.dot(
            jnp.concatenate([high, low], axis=1), mat_ref[index], preferred_element_type=F32
        )
        return out[:, :128] + out[:, 128:]

    def laplace(v):
        high, low = halves(v)
        xy = jnp.dot(
            mat_ref[0], jnp.concatenate([high, low], axis=0), preferred_element_type=F32
        )
        return xy[:128] + xy[128:] + along_z(high, low, 1)

    mass, part, invd = tab_ref.at[0], tab_ref.at[1], tab_ref.at[2]

    def tile_sum(a):
        a = a.reshape(16, 8, 128)
        total = a[0]
        for k in range(1, 16):
            total = total + a[k]
        return total

    def record(slot, total):
        lanes = jnp.sum(total, axis=1, keepdims=True)
        macc[...] += jnp.where(tile_lane == slot, lanes, 0.0)

    loads[0].wait()
    loads[1].wait()
    macc[...] = jnp.zeros_like(macc)
    for e in range(ELEMENTS):
        free[planes(e)] = bnd[planes(e)].astype(F32)
        scaled = mass[...] * inv[planes(e)]
        minv[0, planes(e)] = scaled
        minv[1, planes(e)] = scaled * (1.0 / THERMAL)
        for c in range(4):
            basis[0, c, planes(e)] = jnp.zeros((8, LY, 128), F32)
    loads[2].wait()

    for c in range(4):

        def local_right(e, c=c):
            value = minv[0, planes(e)] * old[c, planes(e)]
            if c == 2:
                value = value + mass[...] * (COUPLING * old[3, planes(e)])
            if c == 3:
                value = value - mass[...] * (STRATIFY * old[2, planes(e)])
            return value

        def emit_right(e, w, c=c):
            basis[1, c, planes(e)] = free[planes(e)] * w
            pack(vsnd.at[0, c], e, w)

        assembled(local_right, emit_right)
        if c == 0:
            pl.semaphore_wait(barrier, greeted)
        send_faces(vsnd.at[0, c], vrcv.at[0, c], vss.at[0, c], vrs.at[0, c])

    shift = CENTRE / HALF

    def krylov(j, last):
        now = lax.rem(j, 2)
        later = 1 - now
        for c in range(4):
            wait_all(vrcv.at[now, c], vrs.at[now, c])
            totals = [jnp.zeros((8, 128), F32)] * 3
            if not last:

                @pl.when(j >= 1)
                def _(c=c):
                    wait_all(vsnd.at[later, c], vss.at[later, c])

            def local(e, c=c, totals=totals):
                v = basis[j + 1, c, planes(e)] + free[planes(e)] * halo(vrcv.at[now, c], e)
                basis[j + 1, c, planes(e)] = v
                weighted = v * part[...]
                totals[0] = totals[0] + tile_sum(weighted * v)
                totals[1] = totals[1] + tile_sum(weighted * basis[j, c, planes(e)])
                lap = laplace(v.reshape(128, 128)).reshape(8, LY, 128)
                w = mass[...] * lap + minv[c // 3, planes(e)] * v
                if last:
                    totals[2] = totals[2] + tile_sum(w * v)
                return w

            def emit(e, w, c=c):
                basis[j + 2, c, planes(e)] = (
                    free[planes(e)] * w
                    - shift * basis[j + 1, c, planes(e)]
                    - basis[j, c, planes(e)]
                )
                pack(vsnd.at[later, c], e, w)

            if last:
                for e in range(ELEMENTS):
                    local(e)
            else:
                assembled(local, emit)
                send_faces(
                    vsnd.at[later, c], vrcv.at[later, c], vss.at[later, c], vrs.at[later, c]
                )
            record(4 * j + c, totals[0])
            record(4 * (ITERS + j) + c, totals[1])
            if last:
                record(4 * 2 * ITERS + c, totals[2])

    def krylov_body(j, carry):
        krylov(j, False)
        return carry

    lax.fori_loop(0, ITERS - 1, krylov_body, 0)
    krylov(jnp.int32(ITERS - 1), True)

    value = jnp.sum(macc[...], axis=0, keepdims=True)
    for k, partners in enumerate(stages):
        arow[k] = value
        copies = []
        for mask, device in partners:
            copy = pltpu.make_async_remote_copy(
                src_ref=arow.at[k],
                dst_ref=arcv.at[k, mask],
                send_sem=ass.at[k, mask],
                recv_sem=ars.at[k, mask],
                device_id=device,
                device_id_type=MESH,
            )
            copy.start()
            copies.append(copy)
        for (mask, _), copy in zip(partners, copies):
            copy.wait_recv()
        for mask, _ in partners:
            value = value + arcv[k, mask]
        for copy in copies:
            copy.wait_send()

    def moment(index):
        return value if index == 0 else pltpu.roll(value, 128 - 4 * index, 1)

    q = [moment(j) for j in range(ITERS)]
    r = [moment(ITERS + j) for j in range(1, ITERS)]
    r.append(moment(2 * ITERS) - shift * q[-1] - r[-1])
    nu = []
    for j in range(ITERS):
        nu.append(q[j] - q[j - 1] if j else q[0])
        nu.append(r[j] - r[j - 1] if j else r[0])

    def gram(i, j):
        total = None
        for k in range(min(i, j) + 1):
            term = nu[abs(i - j) + 2 * k]
            total = term if total is None else total + term
        return total

    system = [[None] * ITERS for _ in range(ITERS)]
    for i in range(ITERS):
        for j in range(i, ITERS):
            entry = shift * gram(i, j) + gram(i, j + 1)
            if j:
                entry = entry + gram(i, j - 1)
            system[i][j] = entry
    right = [nu[i] for i in range(ITERS)]
    inverse = []
    for k in range(ITERS):
        inverse.append(1.0 / system[k][k])
        for i in range(k + 1, ITERS):
            factor = system[k][i] * inverse[k]
            for j in range(i, ITERS):
                system[i][j] = system[i][j] - factor * system[k][j]
            right[i] = right[i] - factor * right[k]
    answer = [None] * ITERS
    for k in reversed(range(ITERS)):
        total = right[k]
        for j in range(k + 1, ITERS):
            total = total - system[k][j] * answer[j]
        answer[k] = total * inverse[k]

    lane_row = lax.broadcasted_iota(jnp.int32, (1, 128), 1)
    for c in range(4):
        weights = []
        for j in range(ITERS):
            one = jnp.sum(jnp.where(lane_row == c, answer[j], 0.0), axis=1, keepdims=True)
            if c == 3:
                one = one * (1.0 / THERMAL)
            weights.append(jnp.broadcast_to(one, (8, 128)).reshape(1, 8, 128))
        for x in range(0, LX, 8):
            for y in range(0, LY, 8):
                where = (pl.ds(x, 8), pl.ds(y, 8))
                total = weights[0] * basis[1, c, where[0], where[1]]
                for j in range(1, ITERS):
                    total = total + weights[j] * basis[j + 1, c, where[0], where[1]]
                fields[c, where[0], where[1]] = total
    store_fields = pltpu.make_async_copy(fields, new_hbm, osem.at[0])
    store_fields.start()

    def local_source(e):
        u0, l0 = halves(fields[0, planes(e)].reshape(128, 128))
        u1, l1 = halves(fields[1, planes(e)].reshape(128, 128))
        u2, l2 = halves(fields[2, planes(e)].reshape(128, 128))
        high = jnp.dot(
            mat_ref[2], jnp.concatenate([u0, u1], axis=0), preferred_element_type=F32
        )
        low = jnp.dot(
            mat_ref[2, pl.ds(0, 128), :],
            jnp.concatenate([l0, l1], axis=0),
            preferred_element_type=F32,
        )
        total = high[:128] + high[128:] + low + along_z(u2, l2, 3)
        return mass[...] * total.reshape(8, LY, 128)

    def emit_source(e, w):
        rem[planes(e)] = -free[planes(e)] * w
        upd[planes(e)] = jnp.zeros((8, LY, 128), F32)
        prs[planes(e)] = jnp.zeros((8, LY, 128), F32)
        pack(psnd.at[0], e, w)

    assembled(local_source, emit_source)
    send_faces(psnd.at[0], prcv.at[0], pss.at[0], prs_sem.at[0])

    pairs = chebyshev_coefficients()

    def refreshed(e, now, keep, gain):
        left = rem[planes(e)] - free[planes(e)] * halo(prcv.at[now], e)
        update = keep * upd[planes(e)] + gain * (invd[...] * left)
        prs[planes(e)] = prs[planes(e)] + update
        return left, update

    def chebyshev_body(i, carry):
        now = lax.rem(i, 2)
        later = 1 - now
        keep, gain = jnp.float32(pairs[0][0]), jnp.float32(pairs[0][1])
        for k in range(1, CHEB - 1):
            keep = jnp.where(i == k, jnp.float32(pairs[k][0]), keep)
            gain = jnp.where(i == k, jnp.float32(pairs[k][1]), gain)
        wait_all(prcv.at[now], prs_sem.at[now])

        @pl.when(i >= 1)
        def _():
            wait_all(psnd.at[later], pss.at[later])

        def local(e):
            left, update = refreshed(e, now, keep, gain)
            rem[planes(e)] = left
            upd[planes(e)] = update
            lap = laplace(update.reshape(128, 128)).reshape(8, LY, 128)
            return mass[...] * (lap + SIGMA_SHIFT * update)

        def emit(e, w):
            rem[planes(e)] = rem[planes(e)] - free[planes(e)] * w
            pack(psnd.at[later], e, w)

        assembled(local, emit)
        send_faces(psnd.at[later], prcv.at[later], pss.at[later], prs_sem.at[later])
        return carry

    lax.fori_loop(0, CHEB - 1, chebyshev_body, 0)
    now = (CHEB - 1) % 2
    wait_all(prcv.at[now], prs_sem.at[now])
    for e in range(ELEMENTS):
        refreshed(e, now, pairs[CHEB - 1][0], pairs[CHEB - 1][1])
    store_pressure = pltpu.make_async_copy(prs, prs_hbm, osem.at[1])
    store_pressure.start()
    for slot in range(2):
        wait_all(psnd.at[slot], pss.at[slot])
        for c in range(4):
            wait_all(vsnd.at[slot, c], vss.at[slot, c])
    store_fields.wait()
    store_pressure.wait()


def solution(mesh):
    nx, ny = mesh.shape["gx"], mesh.shape["gy"]
    stages = reduction_stages(nx, ny)
    most = max(1 << len(bits) for bits in stages)
    matrices = matrix_tables()
    tables = field_tables()
    brick = (LX, LY, LZ)

    def body(*refs):
        step_kernel(nx, ny, *refs)

    def on_device(old_fields, inverse_step, boundary):
        any_space = pl.BlockSpec(memory_space=pl.ANY)
        vmem = pl.BlockSpec(memory_space=pltpu.VMEM)
        return pl.pallas_call(
            body,
            out_shape=(
                jax.ShapeDtypeStruct((4,) + brick, F32),
                jax.ShapeDtypeStruct(brick, F32),
            ),
            in_specs=[any_space] * 3 + [vmem] * 2,
            out_specs=(any_space, any_space),
            scratch_shapes=[
                pltpu.VMEM((4,) + brick, F32),
                pltpu.VMEM(brick, F32),
                pltpu.VMEM(brick, jnp.int32),
                pltpu.VMEM(brick, F32),
                pltpu.VMEM((2,) + brick, F32),
                pltpu.VMEM((ITERS + 1, 4) + brick, F32),
                pltpu.VMEM((4,) + brick, F32),
                pltpu.VMEM(brick, F32),
                pltpu.VMEM(brick, F32),
                pltpu.VMEM(brick, F32),
                pltpu.VMEM((2, 4, 128, 128), F32),
                pltpu.VMEM((2, 4, 128, 128), F32),
                pltpu.VMEM((2, 128, 128), F32),
                pltpu.VMEM((2, 128, 128), F32),
                pltpu.VMEM((8, 128), F32),
                pltpu.VMEM((len(stages), 1, 128), F32),
                pltpu.VMEM((len(stages), most, 1, 128), F32),
                pltpu.SemaphoreType.DMA((3,)),
                pltpu.SemaphoreType.DMA((2, 4)),
                pltpu.SemaphoreType.DMA((2, 4)),
                pltpu.SemaphoreType.DMA((2,)),
                pltpu.SemaphoreType.DMA((2,)),
                pltpu.SemaphoreType.DMA((len(stages), most)),
                pltpu.SemaphoreType.DMA((len(stages), most)),
                pltpu.SemaphoreType.DMA((2,)),
            ],
            compiler_params=pltpu.CompilerParams(
                collective_id=0, has_side_effects=True, vmem_limit_bytes=40 * 1024 * 1024
            ),
        )(old_fields, inverse_step, boundary, jnp.asarray(matrices), jnp.asarray(tables))

    return jax.shard_map(
        on_device,
        mesh=mesh,
        in_specs=(P(None, "gx", "gy", None), P("gx", "gy", None), P("gx", "gy", None)),
        out_specs=(P(None, "gx", "gy", None), P("gx", "gy", None)),
        check_vma=False,
    )
```

```python
import jax
import jax.numpy as jnp
import ml_dtypes
import numpy as np
from jax import lax
from jax.experimental import pallas as pl
from jax.experimental.pallas import tpu as pltpu
from jax.sharding import PartitionSpec as P

ITERS = 6
CHEB = 6
SIGMA_SHIFT = 0.5
THERMAL = 1.4
COUPLING = 1.0
STRATIFY = 1.0
SPREAD = 20.0
CENTRE = 6.0
HALF = 2.9
LOBATTO_POINTS = (
    -1.0,
    -0.8717401485096066,
    -0.5917001814331423,
    -0.2092992179024789,
    0.2092992179024789,
    0.5917001814331423,
    0.8717401485096066,
    1.0,
)
MESH = pl.DeviceIdType.MESH
LX, LY, LZ = 32, 16, 128
ELEMENTS = LX // 8
F32 = jnp.float32
X_FACES = ((-1, 0, 0, 16, 16), (1, 0, 16, 0, 16))
Y_FACES = ((0, -1, 32, 64, 32), (0, 1, 64, 32, 32))
FACE_ROWS = 96
CORNERS = ((-1, -1, 0, 3), (-1, 1, 1, 2), (1, -1, 2, 1), (1, 1, 3, 0))


def legendre_value(points, degree):
    previous = points * 0.0 + 1.0
    current = points
    for order in range(1, degree):
        following = ((2 * order + 1) * points * current - order * previous) / (order + 1)
        previous = current
        current = following
    return current


def quadrature_tables():
    degree = 7
    points = np.array(LOBATTO_POINTS)
    values = legendre_value(points, degree)
    weights = 2.0 / (degree * (degree + 1) * values * values)
    derive = np.zeros((degree + 1, degree + 1))
    for row in range(degree + 1):
        for column in range(degree + 1):
            if row != column:
                derive[row, column] = values[row] / (
                    values[column] * (points[row] - points[column])
                )
    derive[0, 0] = -degree * (degree + 1) / 4.0
    derive[degree, degree] = degree * (degree + 1) / 4.0
    return weights, derive, derive.T @ (weights[:, None] * derive)


def chebyshev_bounds():
    weights, _, stiff = quadrature_tables()
    w = np.diag(weights)
    element = np.kron(np.kron(stiff, w), w)
    element = element + np.kron(np.kron(w, stiff), w)
    element = element + np.kron(np.kron(w, w), stiff)
    element = element + SIGMA_SHIFT * np.kron(np.kron(w, w), w)
    upper = float(np.max(np.sum(np.abs(element), axis=1) / np.diag(element)))
    lower = upper / SPREAD
    return (upper + lower) / 2.0, (upper - lower) / 2.0


def chebyshev_coefficients():
    centre, half = chebyshev_bounds()
    ratio = centre / half
    damping = 1.0 / ratio
    pairs = [(0.0, 1.0 / centre)]
    for _ in range(CHEB - 1):
        following = 1.0 / (2.0 * ratio - damping)
        pairs.append((following * damping, 2.0 * following / half))
        damping = following
    return pairs


def split_pair(matrix):
    high = matrix.astype(ml_dtypes.bfloat16)
    low = (matrix - high.astype(np.float64)).astype(ml_dtypes.bfloat16)
    return high, low


def left_table(matrix):
    high, low = split_pair(matrix)
    return np.block([[high, high], [low, np.zeros_like(low)]])


def right_table(matrix):
    high, low = split_pair(matrix)
    return np.block([[high, low], [high, np.zeros_like(low)]])


def matrix_tables():
    weights, derive, stiff = quadrature_tables()
    scaled = stiff / weights[:, None]
    eye_y = np.eye(LY // 8)
    eye_z = np.eye(LZ // 8)
    lap_xy = np.kron(scaled, np.eye(LY)) + np.kron(np.eye(8), np.kron(eye_y, scaled))
    lap_z = np.kron(eye_z, scaled).T
    div_xy = np.concatenate(
        [np.kron(derive, np.eye(LY)), np.kron(np.eye(8), np.kron(eye_y, derive))], axis=1
    )
    div_z = np.kron(eye_z, derive).T
    return np.stack(
        [
            left_table(lap_xy),
            right_table(lap_z),
            np.concatenate(split_pair(div_xy), axis=0),
            right_table(div_z),
        ]
    )


def field_tables():
    weights, _, stiff = quadrature_tables()
    mass = weights[:, None, None] * np.tile(weights, 2)[None, :, None] * np.tile(weights, 16)
    shared = np.where(np.arange(8) % 7 == 0, 0.5, 1.0)
    shared_z = np.tile(shared, 16)
    shared_z[0] = shared_z[-1] = 1.0
    part = shared[:, None, None] * np.tile(shared, 2)[None, :, None] * shared_z

    def periodic(line):
        line = line.copy()
        line[0] = line[7] = line[0] + line[7]
        return line

    def column(line):
        line = np.tile(line, 16)
        total = line.copy()
        total[8::8] += line[7:-1:8]
        total[7:-1:8] += line[8::8]
        return total

    entry = np.diag(stiff)
    wx, sx = periodic(weights), periodic(entry)
    wy, sy = np.tile(wx, 2), np.tile(sx, 2)
    wz, sz = column(weights), column(entry)

    def outer(a, b, c):
        return a[:, None, None] * b[None, :, None] * c

    diagonal = outer(sx, wy, wz) + outer(wx, sy, wz) + outer(wx, wy, sz)
    diagonal = diagonal + SIGMA_SHIFT * outer(wx, wy, wz)
    return np.stack([mass / HALF, part, HALF / diagonal]).astype(np.float32)


def reduction_stages(nx, ny):
    bits_y = ny.bit_length() - 1
    bits = list(range(bits_y + nx.bit_length() - 1))
    stages = [[b for b in bits if b < 2 or b >= bits_y], [b for b in bits if 2 <= b < bits_y]]
    return [stage for stage in stages if stage]


def step_kernel(nx, ny, *refs):
    (old_hbm, inv_hbm, bnd_hbm, mat_hbm, tab_hbm, new_hbm, prs_hbm) = refs[:7]
    (old, inv, bnd, mat_ref, tab_ref, free, minv, basis, fields, rem, upd, prs) = refs[7:19]
    (vsnd, vrcv, vcsnd, vcrcv, psnd, prcv, pcsnd, pcrcv) = refs[19:27]
    (ssnd, srcv, scsnd, scrcv, hsum, hcsum, macc, arow, arcv) = refs[27:36]
    (lsem, vsem, psem, ssem, ass, ars, osem) = refs[36:]

    gx = lax.axis_index("gx")
    gy = lax.axis_index("gy")

    def neighbour(dx, dy):
        return (lax.rem(gx + dx + nx, nx), lax.rem(gy + dy + ny, ny))

    me = gx * ny + gy
    stages = []
    for bits in reduction_stages(nx, ny):
        partners = []
        for mask in range(1, 1 << len(bits)):
            other = me
            for place, b in enumerate(bits):
                if mask >> place & 1:
                    other = other + (1 - 2 * lax.rem(lax.div(me, 1 << b), 2)) * (1 << b)
            partners.append((mask, (lax.div(other, ny), lax.rem(other, ny))))
        stages.append(partners)

    barrier = pltpu.get_barrier_semaphore()
    greeted = 0
    for dx, dy, *_ in CORNERS + Y_FACES + X_FACES:
        pl.semaphore_signal(barrier, inc=1, device_id=neighbour(dx, dy), device_id_type=MESH)
        greeted += 1
    for partners in stages:
        for _, device in partners:
            pl.semaphore_signal(barrier, inc=1, device_id=device, device_id_type=MESH)
            greeted += 1

    loads = [
        pltpu.make_async_copy(inv_hbm, inv, lsem.at[0]),
        pltpu.make_async_copy(bnd_hbm, bnd, lsem.at[1]),
        pltpu.make_async_copy(tab_hbm, tab_ref, lsem.at[2]),
        pltpu.make_async_copy(old_hbm, old, lsem.at[3]),
        pltpu.make_async_copy(mat_hbm, mat_ref, lsem.at[4]),
    ]
    for load in loads:
        load.start()

    lane = lax.broadcasted_iota(jnp.int32, (128, 128), 1)
    z_first = (lax.rem(lane, 8) == 0) & (lane > 0)
    z_last = (lax.rem(lane, 8) == 7) & (lane < LZ - 1)
    row3 = lax.broadcasted_iota(jnp.int32, (8, 8, 128), 1)
    row3_first, row3_last = row3 == 0, row3 == 7
    row = lax.broadcasted_iota(jnp.int32, (8, 128), 0)
    row_first, row_last = row == 0, row == 7
    tile_lane = lax.broadcasted_iota(jnp.int32, (8, 128), 1)

    def planes(e):
        return pl.ds(8 * e, 8)

    def inner_sums(w):
        flat = w.reshape(128, 128)
        flat = (
            flat
            + jnp.where(z_first, pltpu.roll(flat, 1, 1), 0.0)
            + jnp.where(z_last, pltpu.roll(flat, 127, 1), 0.0)
        )
        w = flat.reshape(8, LY, 128)
        a, b = w[:, :8], w[:, 8:]
        a_sum = a + jnp.where(row3_last, pltpu.roll(b, 7, 1), 0.0)
        b_sum = b + jnp.where(row3_first, pltpu.roll(a, 1, 1), 0.0)
        return jnp.concatenate([a_sum, b_sum], axis=1)

    def assembled(local, emit, ends=None, done=None):
        w0 = inner_sums(local(0))
        w3 = inner_sums(local(3))
        if ends is not None:
            ends(w0, w3)
        w1 = inner_sums(local(1))
        both = w0[7:] + w1[:1]
        emit(0, jnp.concatenate([w0[:7], both], axis=0))
        w1 = jnp.concatenate([both, w1[1:]], axis=0)
        w2 = inner_sums(local(2))
        both = w1[7:] + w2[:1]
        emit(1, jnp.concatenate([w1[:7], both], axis=0))
        w2 = jnp.concatenate([both, w2[1:]], axis=0)
        both = w2[7:] + w3[:1]
        emit(2, jnp.concatenate([w2[:7], both], axis=0))
        emit(3, jnp.concatenate([both, w3[1:]], axis=0))
        if done is not None:
            done()

    class Faces:
        def __init__(self, send, receive, corner_send, corner_receive, sems):
            self.send, self.receive = send, receive
            self.corner_send, self.corner_receive = corner_send, corner_receive
            self.sems = sems

        def post(self, faces):
            for dx, dy, here, there, rows in faces:
                pltpu.make_async_remote_copy(
                    src_ref=self.send.at[pl.ds(here, rows)],
                    dst_ref=self.receive.at[pl.ds(there, rows)],
                    send_sem=self.sems(0),
                    recv_sem=self.sems(1),
                    device_id=neighbour(dx, dy),
                    device_id_type=MESH,
                ).start()

        def ends(self, w0, w3):
            self.corner_send[0] = w0[0, :1]
            self.corner_send[1] = w0[0, LY - 1 :]
            self.corner_send[2] = w3[7, :1]
            self.corner_send[3] = w3[7, LY - 1 :]
            for dx, dy, here, there in CORNERS:
                pltpu.make_async_remote_copy(
                    src_ref=self.corner_send.at[here],
                    dst_ref=self.corner_receive.at[there],
                    send_sem=self.sems(2),
                    recv_sem=self.sems(3),
                    device_id=neighbour(dx, dy),
                    device_id_type=MESH,
                ).start()
            self.send[pl.ds(0, 16), :] = w0[0]
            self.send[pl.ds(16, 16), :] = w3[7]
            self.post(X_FACES)

        def rows(self, e, w):
            self.send[pl.ds(32 + 8 * e, 8), :] = w[:, 0, :]
            self.send[pl.ds(64 + 8 * e, 8), :] = w[:, LY - 1, :]

        def done(self):
            self.post(Y_FACES)

        def arrived(self):
            wait_all(self.receive, self.sems(1))
            wait_all(self.corner_receive, self.sems(3))

        def sent(self):
            wait_all(self.send, self.sems(0))
            wait_all(self.corner_send, self.sems(2))

    def velocity_faces(slot, c):
        return Faces(
            vsnd.at[slot, c],
            vrcv.at[slot, c],
            vcsnd.at[slot, c],
            vcrcv.at[slot, c],
            lambda k: vsem.at[k, slot, c],
        )

    def pressure_faces(slot):
        return Faces(
            psnd.at[slot],
            prcv.at[slot],
            pcsnd.at[slot],
            pcrcv.at[slot],
            lambda k: psem.at[k, slot],
        )

    def source_faces(j, slot, c):
        return Faces(
            ssnd.at[slot, c],
            srcv.at[j, c],
            scsnd.at[slot, c],
            scrcv.at[j, c],
            lambda k: ssem.at[k, j, c],
        )

    def spread_row(line):
        return jnp.broadcast_to(line, (8, 128))

    def halo(faces, corners, e):
        out = []
        for x in range(8):
            first = spread_row(faces[pl.ds(32 + 8 * e + x, 1), :])
            last = spread_row(faces[pl.ds(64 + 8 * e + x, 1), :])
            side = None
            if e == 0 and x == 0:
                side, corner = 0, 0
            if e == ELEMENTS - 1 and x == 7:
                side, corner = 16, 2
            if side is not None:
                first = first + spread_row(corners[corner])
                last = last + spread_row(corners[corner + 1])
            first = jnp.where(row_first, first, 0.0)
            last = jnp.where(row_last, last, 0.0)
            if side is not None:
                first = first + faces[pl.ds(side, 8), :]
                last = last + faces[pl.ds(side + 8, 8), :]
            out.append(jnp.concatenate([first, last], axis=0))
        return jnp.stack(out)

    def wait_all(ref, sem):
        pltpu.make_async_copy(ref, ref, sem).wait()

    def halves(v):
        high = v.astype(jnp.bfloat16)
        return high, (v - high.astype(F32)).astype(jnp.bfloat16)

    def along_z(high, low, index):
        out = jnp.dot(
            jnp.concatenate([high, low], axis=1), mat_ref[index], preferred_element_type=F32
        )
        return out[:, :128] + out[:, 128:]

    def laplace(v):
        high, low = halves(v)
        xy = jnp.dot(
            mat_ref[0], jnp.concatenate([high, low], axis=0), preferred_element_type=F32
        )
        return xy[:128] + xy[128:] + along_z(high, low, 1)

    mass, part, invd = tab_ref.at[0], tab_ref.at[1], tab_ref.at[2]

    def tile_sum(a):
        a = a.reshape(16, 8, 128)
        total = a[0]
        for k in range(1, 16):
            total = total + a[k]
        return total

    def record(slot, total):
        lanes = jnp.sum(total, axis=1, keepdims=True)
        macc[...] += jnp.where(tile_lane == slot, lanes, 0.0)

    for load in loads[:3]:
        load.wait()
    macc[...] = jnp.zeros_like(macc)
    for e in range(ELEMENTS):
        free[planes(e)] = bnd[planes(e)].astype(F32)
        scaled = mass[...] * inv[planes(e)]
        minv[0, planes(e)] = scaled
        minv[1, planes(e)] = scaled * (1.0 / THERMAL)
        for c in range(4):
            basis[0, c, planes(e)] = jnp.zeros((8, LY, 128), F32)
    loads[3].wait()

    for c in range(4):

        def local_right(e, c=c):
            value = minv[0, planes(e)] * old[c, planes(e)]
            if c == 2:
                value = value + mass[...] * (COUPLING * old[3, planes(e)])
            if c == 3:
                value = value - mass[...] * (STRATIFY * old[2, planes(e)])
            return value

        faces = velocity_faces(0, c)

        def emit_right(e, w, c=c, faces=faces):
            basis[1, c, planes(e)] = free[planes(e)] * w
            faces.rows(e, w)

        def ends_right(w0, w3, c=c, faces=faces):
            if c == 0:
                pl.semaphore_wait(barrier, greeted)
            faces.ends(w0, w3)

        assembled(local_right, emit_right, ends_right, faces.done)
    loads[4].wait()

    shift = CENTRE / HALF

    def divergence(c, v):
        high, low = halves(v)
        if c == 2:
            return along_z(high, low, 3)
        out = jnp.dot(
            mat_ref[2, :, pl.ds(128 * c, 128)], high, preferred_element_type=F32
        )
        low = jnp.dot(
            mat_ref[2, pl.ds(0, 128), pl.ds(128 * c, 128)], low, preferred_element_type=F32
        )
        return out[:128] + out[128:] + low

    def source_parts(j):
        slot = lax.rem(j, 2)
        for c in range(3):
            faces = source_faces(j, slot, c)

            @pl.when(j >= 2)
            def _(c=c, slot=slot):
                source_faces(j - 2, slot, c).sent()

            def local(e, c=c):
                v = basis[j + 1, c, planes(e)].reshape(128, 128)
                return mass[...] * divergence(c, v).reshape(8, LY, 128)

            assembled(local, faces.rows, faces.ends, faces.done)

    def krylov(j, last):
        now = lax.rem(j, 2)
        later = 1 - now
        for c in range(4):
            here = velocity_faces(now, c)
            there = velocity_faces(later, c)
            here.arrived()
            totals = [jnp.zeros((8, 128), F32)] * 3
            if not last:

                @pl.when(j >= 1)
                def _(there=there):
                    there.sent()

            def local(e, c=c, totals=totals, here=here):
                v = basis[j + 1, c, planes(e)] + free[planes(e)] * halo(
                    here.receive, here.corner_receive, e
                )
                basis[j + 1, c, planes(e)] = v
                weighted = v * part[...]
                totals[0] = totals[0] + tile_sum(weighted * v)
                totals[1] = totals[1] + tile_sum(weighted * basis[j, c, planes(e)])
                lap = laplace(v.reshape(128, 128)).reshape(8, LY, 128)
                w = mass[...] * lap + minv[c // 3, planes(e)] * v
                if last:
                    totals[2] = totals[2] + tile_sum(w * v)
                return w

            def emit(e, w, c=c, there=there):
                basis[j + 2, c, planes(e)] = (
                    free[planes(e)] * w
                    - shift * basis[j + 1, c, planes(e)]
                    - basis[j, c, planes(e)]
                )
                there.rows(e, w)

            if last:
                for e in range(ELEMENTS):
                    local(e)
            else:
                assembled(local, emit, there.ends, there.done)
            record(4 * j + c, totals[0])
            record(4 * (ITERS + j) + c, totals[1])
            if last:
                record(4 * 2 * ITERS + c, totals[2])

    def krylov_body(j, carry):
        krylov(j, False)
        source_parts(j)
        return carry

    lax.fori_loop(0, ITERS - 1, krylov_body, 0)
    krylov(jnp.int32(ITERS - 1), True)

    value = jnp.sum(macc[...], axis=0, keepdims=True)
    for k, partners in enumerate(stages):
        arow[k] = value
        copies = []
        for mask, device in partners:
            copy = pltpu.make_async_remote_copy(
                src_ref=arow.at[k],
                dst_ref=arcv.at[k, mask],
                send_sem=ass.at[k, mask],
                recv_sem=ars.at[k, mask],
                device_id=device,
                device_id_type=MESH,
            )
            copy.start()
            copies.append(copy)
        if k == 0:
            source_parts(jnp.int32(ITERS - 1))
        for (mask, _), copy in zip(partners, copies):
            copy.wait_recv()
        for mask, _ in partners:
            value = value + arcv[k, mask]
        for copy in copies:
            copy.wait_send()

    def moment(index):
        return value if index == 0 else pltpu.roll(value, 128 - 4 * index, 1)

    q = [moment(j) for j in range(ITERS)]
    r = [moment(ITERS + j) for j in range(1, ITERS)]
    r.append(moment(2 * ITERS) - shift * q[-1] - r[-1])
    nu = []
    for j in range(ITERS):
        nu.append(q[j] - q[j - 1] if j else q[0])
        nu.append(r[j] - r[j - 1] if j else r[0])

    def gram(i, j):
        total = None
        for k in range(min(i, j) + 1):
            term = nu[abs(i - j) + 2 * k]
            total = term if total is None else total + term
        return total

    system = [[None] * ITERS for _ in range(ITERS)]
    for i in range(ITERS):
        for j in range(i, ITERS):
            entry = shift * gram(i, j) + gram(i, j + 1)
            if j:
                entry = entry + gram(i, j - 1)
            system[i][j] = entry
    right = [nu[i] for i in range(ITERS)]
    inverse = []
    for k in range(ITERS):
        inverse.append(1.0 / system[k][k])
        for i in range(k + 1, ITERS):
            factor = system[k][i] * inverse[k]
            for j in range(i, ITERS):
                system[i][j] = system[i][j] - factor * system[k][j]
            right[i] = right[i] - factor * right[k]
    answer = [None] * ITERS
    for k in reversed(range(ITERS)):
        total = right[k]
        for j in range(k + 1, ITERS):
            total = total - system[k][j] * answer[j]
        answer[k] = total * inverse[k]

    lane_row = lax.broadcasted_iota(jnp.int32, (1, 128), 1)

    def coefficients(c):
        out = []
        for j in range(ITERS):
            one = jnp.sum(jnp.where(lane_row == c, answer[j], 0.0), axis=1, keepdims=True)
            if c == 3:
                one = one * (1.0 / THERMAL)
            out.append(jnp.broadcast_to(one, (8, 128)).reshape(1, 8, 128))
        return out

    def combine(c, weights):
        for x in range(0, LX, 8):
            for y in range(0, LY, 8):
                where = (pl.ds(x, 8), pl.ds(y, 8))
                total = weights[0] * basis[1, c, where[0], where[1]]
                for j in range(1, ITERS):
                    total = total + weights[j] * basis[j + 1, c, where[0], where[1]]
                fields[c, where[0], where[1]] = total

    known = [coefficients(c) for c in range(3)]
    for c in range(3):
        combine(c, known[c])

    for c in range(3):
        for j in range(ITERS):
            source_faces(j, j % 2, c).arrived()
    for r in range(0, FACE_ROWS, 8):
        total = None
        for c in range(3):
            for j in range(ITERS):
                term = known[c][j][0] * srcv[j, c, pl.ds(r, 8), :]
                total = term if total is None else total + term
        hsum[pl.ds(r, 8), :] = total
    for k in range(4):
        total = None
        for c in range(3):
            for j in range(ITERS):
                term = known[c][j][0, :1] * scrcv[j, c, k]
                total = term if total is None else total + term
        hcsum[k] = total

    def local_source(e):
        total = None
        for c in range(3):
            term = divergence(c, fields[c, planes(e)].reshape(128, 128))
            total = term if total is None else total + term
        return mass[...] * total.reshape(8, LY, 128)

    pairs = chebyshev_coefficients()

    def emit_source(e, w):
        left = -free[planes(e)] * (w + halo(hsum, hcsum, e))
        update = pairs[0][1] * (invd[...] * left)
        rem[planes(e)] = left
        upd[planes(e)] = update
        prs[planes(e)] = update

    assembled(local_source, emit_source)

    def apply_pressure(local, faces):
        def emit(e, w):
            rem[planes(e)] = rem[planes(e)] - free[planes(e)] * w
            faces.rows(e, w)

        assembled(local, emit, faces.ends, faces.done)

    def operator(update):
        lap = laplace(update.reshape(128, 128)).reshape(8, LY, 128)
        return mass[...] * (lap + SIGMA_SHIFT * update)

    apply_pressure(lambda e: operator(upd[planes(e)]), pressure_faces(0))
    combine(3, coefficients(3))
    store_fields = pltpu.make_async_copy(fields, new_hbm, osem.at[0])
    store_fields.start()

    def refreshed(e, faces, keep, gain):
        left = rem[planes(e)] - free[planes(e)] * halo(faces.receive, faces.corner_receive, e)
        update = keep * upd[planes(e)] + gain * (invd[...] * left)
        prs[planes(e)] = prs[planes(e)] + update
        return left, update

    def chebyshev_body(i, carry):
        now = lax.rem(i + 1, 2)
        here = pressure_faces(now)
        there = pressure_faces(1 - now)
        keep, gain = jnp.float32(pairs[1][0]), jnp.float32(pairs[1][1])
        for k in range(2, CHEB - 1):
            keep = jnp.where(i == k, jnp.float32(pairs[k][0]), keep)
            gain = jnp.where(i == k, jnp.float32(pairs[k][1]), gain)
        here.arrived()

        @pl.when(i >= 2)
        def _():
            there.sent()

        def local(e):
            left, update = refreshed(e, here, keep, gain)
            rem[planes(e)] = left
            upd[planes(e)] = update
            return operator(update)

        apply_pressure(local, there)
        return carry

    lax.fori_loop(1, CHEB - 1, chebyshev_body, 0)
    here = pressure_faces(CHEB % 2)
    here.arrived()
    for e in range(ELEMENTS):
        refreshed(e, here, pairs[CHEB - 1][0], pairs[CHEB - 1][1])
    store_pressure = pltpu.make_async_copy(prs, prs_hbm, osem.at[1])
    store_pressure.start()
    for slot in range(2):
        pressure_faces(slot).sent()
        for c in range(4):
            velocity_faces(slot, c).sent()
        for c in range(3):
            source_faces(ITERS - 2 + slot, slot, c).sent()
    store_fields.wait()
    store_pressure.wait()


def solution(mesh):
    nx, ny = mesh.shape["gx"], mesh.shape["gy"]
    stages = reduction_stages(nx, ny)
    most = max(1 << len(bits) for bits in stages)
    matrices = matrix_tables()
    tables = field_tables()
    brick = (LX, LY, LZ)

    def body(*refs):
        step_kernel(nx, ny, *refs)

    def on_device(old_fields, inverse_step, boundary):
        any_space = pl.BlockSpec(memory_space=pl.ANY)
        return pl.pallas_call(
            body,
            out_shape=(
                jax.ShapeDtypeStruct((4,) + brick, F32),
                jax.ShapeDtypeStruct(brick, F32),
            ),
            in_specs=[any_space] * 5,
            out_specs=(any_space, any_space),
            scratch_shapes=[
                pltpu.VMEM((4,) + brick, F32),
                pltpu.VMEM(brick, F32),
                pltpu.VMEM(brick, jnp.int32),
                pltpu.VMEM(matrices.shape, jnp.bfloat16),
                pltpu.VMEM(tables.shape, F32),
                pltpu.VMEM(brick, F32),
                pltpu.VMEM((2,) + brick, F32),
                pltpu.VMEM((ITERS + 1, 4) + brick, F32),
                pltpu.VMEM((4,) + brick, F32),
                pltpu.VMEM(brick, F32),
                pltpu.VMEM(brick, F32),
                pltpu.VMEM(brick, F32),
                pltpu.VMEM((2, 4, FACE_ROWS, 128), F32),
                pltpu.VMEM((2, 4, FACE_ROWS, 128), F32),
                pltpu.VMEM((2, 4, 4, 1, 128), F32),
                pltpu.VMEM((2, 4, 4, 1, 128), F32),
                pltpu.VMEM((2, FACE_ROWS, 128), F32),
                pltpu.VMEM((2, FACE_ROWS, 128), F32),
                pltpu.VMEM((2, 4, 1, 128), F32),
                pltpu.VMEM((2, 4, 1, 128), F32),
                pltpu.VMEM((2, 3, FACE_ROWS, 128), F32),
                pltpu.VMEM((ITERS, 3, FACE_ROWS, 128), F32),
                pltpu.VMEM((2, 3, 4, 1, 128), F32),
                pltpu.VMEM((ITERS, 3, 4, 1, 128), F32),
                pltpu.VMEM((FACE_ROWS, 128), F32),
                pltpu.VMEM((4, 1, 128), F32),
                pltpu.VMEM((8, 128), F32),
                pltpu.VMEM((len(stages), 1, 128), F32),
                pltpu.VMEM((len(stages), most, 1, 128), F32),
                pltpu.SemaphoreType.DMA((5,)),
                pltpu.SemaphoreType.DMA((4, 2, 4)),
                pltpu.SemaphoreType.DMA((4, 2)),
                pltpu.SemaphoreType.DMA((4, ITERS, 3)),
                pltpu.SemaphoreType.DMA((len(stages), most)),
                pltpu.SemaphoreType.DMA((len(stages), most)),
                pltpu.SemaphoreType.DMA((2,)),
            ],
            compiler_params=pltpu.CompilerParams(
                collective_id=0, has_side_effects=True, vmem_limit_bytes=63 * 1024 * 1024
            ),
        )(old_fields, inverse_step, boundary, jnp.asarray(matrices), jnp.asarray(tables))

    return jax.shard_map(
        on_device,
        mesh=mesh,
        in_specs=(P(None, "gx", "gy", None), P("gx", "gy", None), P("gx", "gy", None)),
        out_specs=(P(None, "gx", "gy", None), P("gx", "gy", None)),
        check_vma=False,
    )
```

```python
import jax
import jax.numpy as jnp
import ml_dtypes
import numpy as np
from jax import lax
from jax.experimental import pallas as pl
from jax.experimental.pallas import tpu as pltpu
from jax.sharding import PartitionSpec as P

ITERS = 6
CHEB = 6
SIGMA_SHIFT = 0.5
THERMAL = 1.4
COUPLING = 1.0
STRATIFY = 1.0
SPREAD = 20.0
CENTRE = 6.0
HALF = 2.9
LOBATTO_POINTS = (
    -1.0,
    -0.8717401485096066,
    -0.5917001814331423,
    -0.2092992179024789,
    0.2092992179024789,
    0.5917001814331423,
    0.8717401485096066,
    1.0,
)
MESH = pl.DeviceIdType.MESH
LX, LY, LZ = 32, 16, 128
ELEMENTS = LX // 8
F32 = jnp.float32
X_FACES = ((-1, 0, 0, 16, 16), (1, 0, 16, 0, 16))
Y_FACES = ((0, -1, 32, 64, 32), (0, 1, 64, 32, 32))
FACE_ROWS = 96
CORNERS = ((-1, -1, 0, 3), (-1, 1, 1, 2), (1, -1, 2, 1), (1, 1, 3, 0))


def legendre_value(points, degree):
    previous = points * 0.0 + 1.0
    current = points
    for order in range(1, degree):
        following = ((2 * order + 1) * points * current - order * previous) / (order + 1)
        previous = current
        current = following
    return current


def quadrature_tables():
    degree = 7
    points = np.array(LOBATTO_POINTS)
    values = legendre_value(points, degree)
    weights = 2.0 / (degree * (degree + 1) * values * values)
    derive = np.zeros((degree + 1, degree + 1))
    for row in range(degree + 1):
        for column in range(degree + 1):
            if row != column:
                derive[row, column] = values[row] / (
                    values[column] * (points[row] - points[column])
                )
    derive[0, 0] = -degree * (degree + 1) / 4.0
    derive[degree, degree] = degree * (degree + 1) / 4.0
    return weights, derive, derive.T @ (weights[:, None] * derive)


def chebyshev_bounds():
    weights, _, stiff = quadrature_tables()
    w = np.diag(weights)
    element = np.kron(np.kron(stiff, w), w)
    element = element + np.kron(np.kron(w, stiff), w)
    element = element + np.kron(np.kron(w, w), stiff)
    element = element + SIGMA_SHIFT * np.kron(np.kron(w, w), w)
    upper = float(np.max(np.sum(np.abs(element), axis=1) / np.diag(element)))
    lower = upper / SPREAD
    return (upper + lower) / 2.0, (upper - lower) / 2.0


def chebyshev_coefficients():
    centre, half = chebyshev_bounds()
    ratio = centre / half
    damping = 1.0 / ratio
    pairs = [(0.0, 1.0 / centre)]
    for _ in range(CHEB - 1):
        following = 1.0 / (2.0 * ratio - damping)
        pairs.append((following * damping, 2.0 * following / half))
        damping = following
    return pairs


def split_pair(matrix):
    high = matrix.astype(ml_dtypes.bfloat16)
    low = (matrix - high.astype(np.float64)).astype(ml_dtypes.bfloat16)
    return high, low


def left_table(matrix):
    high, low = split_pair(matrix)
    return np.block([[high, high], [low, np.zeros_like(low)]])


def right_table(matrix):
    high, low = split_pair(matrix)
    return np.block([[high, low], [high, np.zeros_like(low)]])


def matrix_tables():
    weights, derive, stiff = quadrature_tables()
    scaled = stiff / weights[:, None]
    eye_y = np.eye(LY // 8)
    eye_z = np.eye(LZ // 8)
    lap_xy = np.kron(scaled, np.eye(LY)) + np.kron(np.eye(8), np.kron(eye_y, scaled))
    lap_z = np.kron(eye_z, scaled).T
    div_xy = np.concatenate(
        [np.kron(derive, np.eye(LY)), np.kron(np.eye(8), np.kron(eye_y, derive))], axis=1
    )
    div_z = np.kron(eye_z, derive).T
    return np.stack(
        [
            left_table(lap_xy),
            right_table(lap_z),
            np.concatenate(split_pair(div_xy), axis=0),
            right_table(div_z),
        ]
    )


def field_tables():
    weights, _, stiff = quadrature_tables()
    mass = weights[:, None, None] * np.tile(weights, 2)[None, :, None] * np.tile(weights, 16)
    shared = np.where(np.arange(8) % 7 == 0, 0.5, 1.0)
    shared_z = np.tile(shared, 16)
    shared_z[0] = shared_z[-1] = 1.0
    part = shared[:, None, None] * np.tile(shared, 2)[None, :, None] * shared_z

    def periodic(line):
        line = line.copy()
        line[0] = line[7] = line[0] + line[7]
        return line

    def column(line):
        line = np.tile(line, 16)
        total = line.copy()
        total[8::8] += line[7:-1:8]
        total[7:-1:8] += line[8::8]
        return total

    entry = np.diag(stiff)
    wx, sx = periodic(weights), periodic(entry)
    wy, sy = np.tile(wx, 2), np.tile(sx, 2)
    wz, sz = column(weights), column(entry)

    def outer(a, b, c):
        return a[:, None, None] * b[None, :, None] * c

    diagonal = outer(sx, wy, wz) + outer(wx, sy, wz) + outer(wx, wy, sz)
    diagonal = diagonal + SIGMA_SHIFT * outer(wx, wy, wz)
    return np.stack([mass / HALF, part, HALF / diagonal]).astype(np.float32)


def reduction_stages(nx, ny):
    bits_y = ny.bit_length() - 1
    bits = list(range(bits_y + nx.bit_length() - 1))
    first = [b for b in bits if b == 1 or b >= bits_y]
    stages = [first, [b for b in bits if b not in first]]
    return [stage for stage in stages if stage]


def step_kernel(nx, ny, *refs):
    (old_hbm, inv_hbm, bnd_hbm, mat_hbm, tab_hbm, fields, prs) = refs[:7]
    (old, inv, bnd, mat_ref, tab_ref, free, minv, basis, rem, upd) = refs[7:17]
    (vsnd, vrcv, vcsnd, vcrcv, psnd, prcv, pcsnd, pcrcv) = refs[17:25]
    (ssnd, srcv, scsnd, scrcv, hsum, hcsum, macc, arow, arcv) = refs[25:34]
    (lsem, vsem, psem, ssem, ass, ars) = refs[34:]

    gx = lax.axis_index("gx")
    gy = lax.axis_index("gy")

    def neighbour(dx, dy):
        return (lax.rem(gx + dx + nx, nx), lax.rem(gy + dy + ny, ny))

    me = gx * ny + gy
    bits_y = ny.bit_length() - 1

    def hops(b):
        if b < 2:
            return 2 * b
        return 1 << (b - 2) if b < bits_y else max(1, b - bits_y)

    stages = []
    for bits in reduction_stages(nx, ny):
        partners = []
        masks = range(1, 1 << len(bits))
        masks = sorted(masks, key=lambda m: -sum(hops(b) for i, b in enumerate(bits) if m >> i & 1))
        for mask in masks:
            other = me
            for place, b in enumerate(bits):
                if mask >> place & 1:
                    other = other + (1 - 2 * lax.rem(lax.div(me, 1 << b), 2)) * (1 << b)
            partners.append((mask, (lax.div(other, ny), lax.rem(other, ny))))
        stages.append(partners)

    barrier = pltpu.get_barrier_semaphore()
    greeted = 0
    for dx, dy, *_ in CORNERS + Y_FACES + X_FACES:
        pl.semaphore_signal(barrier, inc=1, device_id=neighbour(dx, dy), device_id_type=MESH)
        greeted += 1
    for partners in stages:
        for _, device in partners:
            pl.semaphore_signal(barrier, inc=1, device_id=device, device_id_type=MESH)
            greeted += 1

    loads = [
        pltpu.make_async_copy(inv_hbm, inv, lsem.at[0]),
        pltpu.make_async_copy(bnd_hbm, bnd, lsem.at[1]),
        pltpu.make_async_copy(tab_hbm, tab_ref, lsem.at[2]),
        pltpu.make_async_copy(old_hbm, old, lsem.at[3]),
        pltpu.make_async_copy(mat_hbm, mat_ref, lsem.at[4]),
    ]
    for load in loads:
        load.start()

    lane = lax.broadcasted_iota(jnp.int32, (128, 128), 1)
    z_first = (lax.rem(lane, 8) == 0) & (lane > 0)
    z_last = (lax.rem(lane, 8) == 7) & (lane < LZ - 1)
    row3 = lax.broadcasted_iota(jnp.int32, (8, 8, 128), 1)
    row3_first, row3_last = row3 == 0, row3 == 7
    row = lax.broadcasted_iota(jnp.int32, (8, 128), 0)
    row_first, row_last = row == 0, row == 7
    tile_lane = lax.broadcasted_iota(jnp.int32, (8, 128), 1)

    def planes(e):
        return pl.ds(8 * e, 8)

    def inner_sums(w):
        flat = w.reshape(128, 128)
        flat = (
            flat
            + jnp.where(z_first, pltpu.roll(flat, 1, 1), 0.0)
            + jnp.where(z_last, pltpu.roll(flat, 127, 1), 0.0)
        )
        w = flat.reshape(8, LY, 128)
        a, b = w[:, :8], w[:, 8:]
        a_sum = a + jnp.where(row3_last, pltpu.roll(b, 7, 1), 0.0)
        b_sum = b + jnp.where(row3_first, pltpu.roll(a, 1, 1), 0.0)
        return jnp.concatenate([a_sum, b_sum], axis=1)

    def assembled(local, emit, ends=None, done=None):
        w0 = inner_sums(local(0))
        w3 = inner_sums(local(3))
        if ends is not None:
            ends(w0, w3)
        w1 = inner_sums(local(1))
        both = w0[7:] + w1[:1]
        emit(0, jnp.concatenate([w0[:7], both], axis=0))
        w1 = jnp.concatenate([both, w1[1:]], axis=0)
        w2 = inner_sums(local(2))
        both = w1[7:] + w2[:1]
        emit(1, jnp.concatenate([w1[:7], both], axis=0))
        w2 = jnp.concatenate([both, w2[1:]], axis=0)
        both = w2[7:] + w3[:1]
        emit(2, jnp.concatenate([w2[:7], both], axis=0))
        emit(3, jnp.concatenate([both, w3[1:]], axis=0))
        if done is not None:
            done()

    class Faces:
        def __init__(self, send, receive, corner_send, corner_receive, sems):
            self.send, self.receive = send, receive
            self.corner_send, self.corner_receive = corner_send, corner_receive
            self.sems = sems

        def start(self, source, target, dx, dy, k):
            pltpu.make_async_remote_copy(
                src_ref=source,
                dst_ref=target,
                send_sem=self.sems(k),
                recv_sem=self.sems(k + 1),
                device_id=neighbour(dx, dy),
                device_id_type=MESH,
            ).start()

        def post(self, faces):
            for dx, dy, here, there, rows in faces:
                here, there = pl.ds(here, rows), pl.ds(there, rows)
                if len(self.send.shape) == 3:
                    source, target = self.send.at[:, here], self.receive.at[:, there]
                else:
                    source, target = self.send.at[here], self.receive.at[there]
                self.start(source, target, dx, dy, 0)

        def post_corners(self):
            for dx, dy, here, there in CORNERS:
                if len(self.send.shape) == 3:
                    source, target = self.corner_send.at[:, here], self.corner_receive.at[:, there]
                else:
                    source, target = self.corner_send.at[here], self.corner_receive.at[there]
                self.start(source, target, dx, dy, 2)

        def field(self, c):
            return Faces(
                self.send.at[c],
                self.receive.at[c],
                self.corner_send.at[c],
                self.corner_receive.at[c],
                self.sems,
            )

        def keep_corners(self, w0, w3):
            self.corner_send[0] = w0[0, :1]
            self.corner_send[1] = w0[0, LY - 1 :]
            self.corner_send[2] = w3[7, :1]
            self.corner_send[3] = w3[7, LY - 1 :]

        def keep_sides(self, w0, w3):
            self.send[pl.ds(0, 16), :] = w0[0]
            self.send[pl.ds(16, 16), :] = w3[7]

        def keep_ends(self, w0, w3):
            self.keep_corners(w0, w3)
            self.keep_sides(w0, w3)

        def ends(self, w0, w3):
            self.keep_corners(w0, w3)
            self.post_corners()
            self.keep_sides(w0, w3)
            self.post(X_FACES)

        def rows(self, e, w):
            self.send[pl.ds(32 + 8 * e, 8), :] = w[:, 0, :]
            self.send[pl.ds(64 + 8 * e, 8), :] = w[:, LY - 1, :]

        def done(self):
            self.post(Y_FACES)

        def post_all(self):
            self.post_corners()
            self.post(Y_FACES + X_FACES)

        def arrived(self):
            wait_all(self.receive, self.sems(1))
            wait_all(self.corner_receive, self.sems(3))

        def sent(self):
            wait_all(self.send, self.sems(0))
            wait_all(self.corner_send, self.sems(2))

    def velocity_faces(slot, c):
        return Faces(
            vsnd.at[slot, c],
            vrcv.at[slot, c],
            vcsnd.at[slot, c],
            vcrcv.at[slot, c],
            lambda k: vsem.at[k, slot, c],
        )

    def pressure_faces(slot):
        return Faces(
            psnd.at[slot],
            prcv.at[slot],
            pcsnd.at[slot],
            pcrcv.at[slot],
            lambda k: psem.at[k, slot],
        )

    def source_faces(j):
        return Faces(
            ssnd.at[j], srcv.at[j], scsnd.at[j], scrcv.at[j], lambda k: ssem.at[k, j]
        )

    def spread_row(line):
        return jnp.broadcast_to(line, (8, 128))

    def halo(faces, corners, e):
        out = []
        for x in range(8):
            first = spread_row(faces[pl.ds(32 + 8 * e + x, 1), :])
            last = spread_row(faces[pl.ds(64 + 8 * e + x, 1), :])
            side = None
            if e == 0 and x == 0:
                side, corner = 0, 0
            if e == ELEMENTS - 1 and x == 7:
                side, corner = 16, 2
            if side is not None:
                first = first + spread_row(corners[corner])
                last = last + spread_row(corners[corner + 1])
            first = jnp.where(row_first, first, 0.0)
            last = jnp.where(row_last, last, 0.0)
            if side is not None:
                first = first + faces[pl.ds(side, 8), :]
                last = last + faces[pl.ds(side + 8, 8), :]
            out.append(jnp.concatenate([first, last], axis=0))
        return jnp.stack(out)

    def wait_all(ref, sem):
        pltpu.make_async_copy(ref, ref, sem).wait()

    def halves(v):
        high = v.astype(jnp.bfloat16)
        return high, (v - high.astype(F32)).astype(jnp.bfloat16)

    def along_z(high, low, index):
        out = jnp.dot(
            jnp.concatenate([high, low], axis=1), mat_ref[index], preferred_element_type=F32
        )
        return out[:, :128] + out[:, 128:]

    def laplace(v):
        high, low = halves(v)
        xy = jnp.dot(
            mat_ref[0], jnp.concatenate([high, low], axis=0), preferred_element_type=F32
        )
        return xy[:128] + xy[128:] + along_z(high, low, 1)

    mass, part, invd = tab_ref.at[0], tab_ref.at[1], tab_ref.at[2]

    def tile_sum(a):
        a = a.reshape(16, 8, 128)
        total = a[0]
        for k in range(1, 16):
            total = total + a[k]
        return total

    def record(slot, total):
        lanes = jnp.sum(total, axis=1, keepdims=True)
        macc[...] += jnp.where(tile_lane == slot, lanes, 0.0)

    for load in loads[:3]:
        load.wait()
    macc[...] = jnp.zeros_like(macc)
    for e in range(ELEMENTS):
        free[planes(e)] = bnd[planes(e)].astype(F32)
        scaled = mass[...] * inv[planes(e)]
        minv[0, planes(e)] = scaled
        minv[1, planes(e)] = scaled * (1.0 / THERMAL)
        for c in range(4):
            basis[0, c, planes(e)] = jnp.zeros((8, LY, 128), F32)
    loads[3].wait()

    for c in range(4):

        def local_right(e, c=c):
            value = minv[0, planes(e)] * old[c, planes(e)]
            if c == 2:
                value = value + mass[...] * (COUPLING * old[3, planes(e)])
            if c == 3:
                value = value - mass[...] * (STRATIFY * old[2, planes(e)])
            return value

        faces = velocity_faces(0, c)

        def emit_right(e, w, c=c, faces=faces):
            basis[1, c, planes(e)] = free[planes(e)] * w
            faces.rows(e, w)

        def ends_right(w0, w3, c=c, faces=faces):
            if c == 0:
                pl.semaphore_wait(barrier, greeted)
            faces.ends(w0, w3)

        assembled(local_right, emit_right, ends_right, faces.done)
    loads[4].wait()

    shift = CENTRE / HALF

    def divergence(c, v):
        high, low = halves(v)
        if c == 2:
            return along_z(high, low, 3)
        out = jnp.dot(
            mat_ref[2, :, pl.ds(128 * c, 128)], high, preferred_element_type=F32
        )
        low = jnp.dot(
            mat_ref[2, pl.ds(0, 128), pl.ds(128 * c, 128)], low, preferred_element_type=F32
        )
        return out[:128] + out[128:] + low

    pairs = chebyshev_coefficients()

    def operator(update):
        lap = laplace(update.reshape(128, 128)).reshape(8, LY, 128)
        return mass[...] * (lap + SIGMA_SHIFT * update)

    def source_parts(j):
        group = source_faces(j)
        for c in range(3):
            faces = group.field(c)

            def local(e, c=c):
                v = basis[j + 1, c, planes(e)]
                return mass[...] * divergence(c, v.reshape(128, 128)).reshape(8, LY, 128)

            assembled(local, faces.rows, faces.keep_ends)
        group.post_all()

    def krylov(j, last):
        now = lax.rem(j, 2)
        later = 1 - now
        for c in range(4):
            here = velocity_faces(now, c)
            there = velocity_faces(later, c)
            here.arrived()
            totals = [jnp.zeros((8, 128), F32)] * 3
            if not last:

                @pl.when(j >= 1)
                def _(there=there):
                    there.sent()

            def local(e, c=c, totals=totals, here=here):
                v = basis[j + 1, c, planes(e)] + free[planes(e)] * halo(
                    here.receive, here.corner_receive, e
                )
                basis[j + 1, c, planes(e)] = v
                weighted = v * part[...]
                totals[0] = totals[0] + tile_sum(weighted * v)
                totals[1] = totals[1] + tile_sum(weighted * basis[j, c, planes(e)])
                lap = laplace(v.reshape(128, 128)).reshape(8, LY, 128)
                w = mass[...] * lap + minv[c // 3, planes(e)] * v
                if last:
                    totals[2] = totals[2] + tile_sum(w * v)
                return w

            def emit(e, w, c=c, there=there):
                basis[j + 2, c, planes(e)] = (
                    free[planes(e)] * w
                    - shift * basis[j + 1, c, planes(e)]
                    - basis[j, c, planes(e)]
                )
                there.rows(e, w)

            if last:
                for e in range(ELEMENTS):
                    local(e)
            else:
                assembled(local, emit, there.ends, there.done)
            record(4 * j + c, totals[0])
            record(4 * (ITERS + j) + c, totals[1])
            if last:
                record(4 * 2 * ITERS + c, totals[2])

    def krylov_body(j, carry):
        krylov(j, False)

        source_parts(j)
        return carry

    lax.fori_loop(0, ITERS - 1, krylov_body, 0)
    krylov(jnp.int32(ITERS - 1), True)

    value = jnp.sum(macc[...], axis=0, keepdims=True)
    for k, partners in enumerate(stages):
        arow[k] = value
        copies = []
        for mask, device in partners:
            copy = pltpu.make_async_remote_copy(
                src_ref=arow.at[k],
                dst_ref=arcv.at[k, mask],
                send_sem=ass.at[k, mask],
                recv_sem=ars.at[k, mask],
                device_id=device,
                device_id_type=MESH,
            )
            copy.start()
            copies.append(copy)
        if k == 0:
            source_parts(jnp.int32(ITERS - 1))
        for (mask, _), copy in zip(partners, copies):
            copy.wait_recv()
        for mask, _ in partners:
            value = value + arcv[k, mask]
        for copy in copies:
            copy.wait_send()

    def moment(index):
        return value if index == 0 else pltpu.roll(value, 128 - 4 * index, 1)

    q = [moment(j) for j in range(ITERS)]
    r = [moment(ITERS + j) for j in range(1, ITERS)]
    r.append(moment(2 * ITERS) - shift * q[-1] - r[-1])
    nu = []
    for j in range(ITERS):
        nu.append(q[j] - q[j - 1] if j else q[0])
        nu.append(r[j] - r[j - 1] if j else r[0])

    def gram(i, j):
        total = None
        for k in range(min(i, j) + 1):
            term = nu[abs(i - j) + 2 * k]
            total = term if total is None else total + term
        return total

    system = [[None] * ITERS for _ in range(ITERS)]
    for i in range(ITERS):
        for j in range(i, ITERS):
            entry = shift * gram(i, j) + gram(i, j + 1)
            if j:
                entry = entry + gram(i, j - 1)
            system[i][j] = entry
    right = [nu[i] for i in range(ITERS)]
    inverse = []
    for k in range(ITERS):
        inverse.append(1.0 / system[k][k])
        for i in range(k + 1, ITERS):
            factor = system[k][i] * inverse[k]
            for j in range(i, ITERS):
                system[i][j] = system[i][j] - factor * system[k][j]
            right[i] = right[i] - factor * right[k]
    answer = [None] * ITERS
    for k in reversed(range(ITERS)):
        total = right[k]
        for j in range(k + 1, ITERS):
            total = total - system[k][j] * answer[j]
        answer[k] = total * inverse[k]

    lane_row = lax.broadcasted_iota(jnp.int32, (1, 128), 1)

    def coefficients(c):
        out = []
        for j in range(ITERS):
            one = jnp.sum(jnp.where(lane_row == c, answer[j], 0.0), axis=1, keepdims=True)
            if c == 3:
                one = one * (1.0 / THERMAL)
            out.append(jnp.broadcast_to(one, (8, 128)).reshape(1, 8, 128))
        return out

    def combine(c, weights):
        for x in range(0, LX, 8):
            for y in range(0, LY, 8):
                where = (pl.ds(x, 8), pl.ds(y, 8))
                total = weights[0] * basis[1, c, where[0], where[1]]
                for j in range(1, ITERS):
                    total = total + weights[j] * basis[j + 1, c, where[0], where[1]]
                fields[c, where[0], where[1]] = total

    known = [coefficients(c) for c in range(3)]
    for c in range(3):
        combine(c, known[c])

    for j in range(ITERS):
        source_faces(j).arrived()
    for r in range(0, FACE_ROWS, 8):
        total = None
        for c in range(3):
            for j in range(ITERS):
                term = known[c][j][0] * srcv[j, c, pl.ds(r, 8), :]
                total = term if total is None else total + term
        hsum[pl.ds(r, 8), :] = total
    for k in range(4):
        total = None
        for c in range(3):
            for j in range(ITERS):
                term = known[c][j][0, :1] * scrcv[j, c, k]
                total = term if total is None else total + term
        hcsum[k] = total

    def local_source(e):
        total = None
        for c in range(3):
            term = divergence(c, fields[c, planes(e)].reshape(128, 128))
            total = term if total is None else total + term
        return mass[...] * total.reshape(8, LY, 128)

    def emit_source(e, w):
        left = -free[planes(e)] * (w + halo(hsum, hcsum, e))
        update = pairs[0][1] * (invd[...] * left)
        rem[planes(e)] = left
        upd[planes(e)] = update
        prs[planes(e)] = update

    def apply_pressure(local, faces):
        def emit(e, w):
            rem[planes(e)] = rem[planes(e)] - free[planes(e)] * w
            faces.rows(e, w)

        assembled(local, emit, faces.ends, faces.done)

    assembled(local_source, emit_source)
    apply_pressure(lambda e: operator(upd[planes(e)]), pressure_faces(0))
    combine(3, coefficients(3))

    def refreshed(e, faces, keep, gain):
        left = rem[planes(e)] - free[planes(e)] * halo(faces.receive, faces.corner_receive, e)
        update = keep * upd[planes(e)] + gain * (invd[...] * left)
        prs[planes(e)] = prs[planes(e)] + update
        return left, update

    def chebyshev_body(i, carry):
        now = lax.rem(i + 1, 2)
        here = pressure_faces(now)
        there = pressure_faces(1 - now)
        keep, gain = jnp.float32(pairs[1][0]), jnp.float32(pairs[1][1])
        for k in range(2, CHEB - 1):
            keep = jnp.where(i == k, jnp.float32(pairs[k][0]), keep)
            gain = jnp.where(i == k, jnp.float32(pairs[k][1]), gain)

        here.arrived()

        @pl.when(i >= 2)
        def _():
            there.sent()

        def local(e):
            left, update = refreshed(e, here, keep, gain)
            rem[planes(e)] = left
            upd[planes(e)] = update
            return operator(update)

        apply_pressure(local, there)
        return carry

    lax.fori_loop(1, CHEB - 1, chebyshev_body, 0)
    here = pressure_faces(CHEB % 2)
    here.arrived()
    for e in range(ELEMENTS):
        refreshed(e, here, pairs[CHEB - 1][0], pairs[CHEB - 1][1])
    for slot in range(2):
        pressure_faces(slot).sent()
        for c in range(4):
            velocity_faces(slot, c).sent()
    for j in range(ITERS):
        source_faces(j).sent()


def store_kernel(fields, pressure, new_hbm, prs_hbm, sems):
    stores = [
        pltpu.make_async_copy(fields, new_hbm, sems.at[0]),
        pltpu.make_async_copy(pressure, prs_hbm, sems.at[1]),
    ]
    for store in stores:
        store.start()
    for store in stores:
        store.wait()


def solution(mesh):
    nx, ny = mesh.shape["gx"], mesh.shape["gy"]
    stages = reduction_stages(nx, ny)
    most = max(1 << len(bits) for bits in stages)
    matrices = matrix_tables()
    tables = field_tables()
    brick = (LX, LY, LZ)

    def body(*refs):
        step_kernel(nx, ny, *refs)

    def on_device(old_fields, inverse_step, boundary):
        any_space = pl.BlockSpec(memory_space=pl.ANY)
        operands = (old_fields, inverse_step, boundary, jnp.asarray(matrices), jnp.asarray(tables))
        operands = [pltpu.with_memory_space_constraint(x, pltpu.HBM) for x in operands]
        results = pl.pallas_call(
            body,
            out_shape=(pltpu.VMEM((4,) + brick, F32), pltpu.VMEM(brick, F32)),
            in_specs=[any_space] * 5,
            out_specs=(pl.BlockSpec(memory_space=pltpu.VMEM),) * 2,
            scratch_shapes=[
                pltpu.VMEM((4,) + brick, F32),
                pltpu.VMEM(brick, F32),
                pltpu.VMEM(brick, jnp.int32),
                pltpu.VMEM(matrices.shape, jnp.bfloat16),
                pltpu.VMEM(tables.shape, F32),
                pltpu.VMEM(brick, F32),
                pltpu.VMEM((2,) + brick, F32),
                pltpu.VMEM((ITERS + 1, 4) + brick, F32),
                pltpu.VMEM(brick, F32),
                pltpu.VMEM(brick, F32),
                pltpu.VMEM((2, 4, FACE_ROWS, 128), F32),
                pltpu.VMEM((2, 4, FACE_ROWS, 128), F32),
                pltpu.VMEM((2, 4, 4, 1, 128), F32),
                pltpu.VMEM((2, 4, 4, 1, 128), F32),
                pltpu.VMEM((2, FACE_ROWS, 128), F32),
                pltpu.VMEM((2, FACE_ROWS, 128), F32),
                pltpu.VMEM((2, 4, 1, 128), F32),
                pltpu.VMEM((2, 4, 1, 128), F32),
                pltpu.VMEM((ITERS, 3, FACE_ROWS, 128), F32),
                pltpu.VMEM((ITERS, 3, FACE_ROWS, 128), F32),
                pltpu.VMEM((ITERS, 3, 4, 1, 128), F32),
                pltpu.VMEM((ITERS, 3, 4, 1, 128), F32),
                pltpu.VMEM((FACE_ROWS, 128), F32),
                pltpu.VMEM((4, 1, 128), F32),
                pltpu.VMEM((8, 128), F32),
                pltpu.VMEM((len(stages), 1, 128), F32),
                pltpu.VMEM((len(stages), most, 1, 128), F32),
                pltpu.SemaphoreType.DMA((5,)),
                pltpu.SemaphoreType.DMA((4, 2, 4)),
                pltpu.SemaphoreType.DMA((4, 2)),
                pltpu.SemaphoreType.DMA((4, ITERS)),
                pltpu.SemaphoreType.DMA((len(stages), most)),
                pltpu.SemaphoreType.DMA((len(stages), most)),
            ],
            compiler_params=pltpu.CompilerParams(
                collective_id=0, has_side_effects=True, vmem_limit_bytes=40 * 1024 * 1024
            ),
        )(*operands)
        results = [pltpu.with_memory_space_constraint(x, pltpu.VMEM) for x in results]
        return pl.pallas_call(
            store_kernel,
            out_shape=(
                jax.ShapeDtypeStruct((4,) + brick, F32),
                jax.ShapeDtypeStruct(brick, F32),
            ),
            in_specs=[any_space] * 2,
            out_specs=(any_space, any_space),
            scratch_shapes=[pltpu.SemaphoreType.DMA((2,))],
            compiler_params=pltpu.CompilerParams(vmem_limit_bytes=8 * 1024 * 1024),
        )(*results)

    return jax.shard_map(
        on_device,
        mesh=mesh,
        in_specs=(P(None, "gx", "gy", None), P("gx", "gy", None), P("gx", "gy", None)),
        out_specs=(P(None, "gx", "gy", None), P("gx", "gy", None)),
        check_vma=False,
    )
```

```python
import jax
import jax.numpy as jnp
import ml_dtypes
import numpy as np
from jax import lax
from jax.experimental import pallas as pl
from jax.experimental.pallas import tpu as pltpu
from jax.sharding import PartitionSpec as P

ITERS = 6
CHEB = 6
SIGMA_SHIFT = 0.5
THERMAL = 1.4
COUPLING = 1.0
STRATIFY = 1.0
SPREAD = 20.0
CENTRE = 6.0
HALF = 2.9
LOBATTO_POINTS = (
    -1.0,
    -0.8717401485096066,
    -0.5917001814331423,
    -0.2092992179024789,
    0.2092992179024789,
    0.5917001814331423,
    0.8717401485096066,
    1.0,
)
MESH = pl.DeviceIdType.MESH
LX, LY, LZ = 32, 16, 128
ELEMENTS = LX // 8
F32 = jnp.float32
X_FACES = ((-1, 0, 0, 16, 16), (1, 0, 16, 0, 16))
Y_FACES = ((0, -1, 32, 64, 32), (0, 1, 64, 32, 32))
FACE_ROWS = 96
CORNERS = ((-1, -1, 0, 3), (-1, 1, 1, 2), (1, -1, 2, 1), (1, 1, 3, 0))


def legendre_value(points, degree):
    previous = points * 0.0 + 1.0
    current = points
    for order in range(1, degree):
        following = ((2 * order + 1) * points * current - order * previous) / (order + 1)
        previous = current
        current = following
    return current


def quadrature_tables():
    degree = 7
    points = np.array(LOBATTO_POINTS)
    values = legendre_value(points, degree)
    weights = 2.0 / (degree * (degree + 1) * values * values)
    derive = np.zeros((degree + 1, degree + 1))
    for row in range(degree + 1):
        for column in range(degree + 1):
            if row != column:
                derive[row, column] = values[row] / (
                    values[column] * (points[row] - points[column])
                )
    derive[0, 0] = -degree * (degree + 1) / 4.0
    derive[degree, degree] = degree * (degree + 1) / 4.0
    return weights, derive, derive.T @ (weights[:, None] * derive)


def chebyshev_bounds():
    weights, _, stiff = quadrature_tables()
    w = np.diag(weights)
    element = np.kron(np.kron(stiff, w), w)
    element = element + np.kron(np.kron(w, stiff), w)
    element = element + np.kron(np.kron(w, w), stiff)
    element = element + SIGMA_SHIFT * np.kron(np.kron(w, w), w)
    upper = float(np.max(np.sum(np.abs(element), axis=1) / np.diag(element)))
    lower = upper / SPREAD
    return (upper + lower) / 2.0, (upper - lower) / 2.0


def chebyshev_coefficients():
    centre, half = chebyshev_bounds()
    ratio = centre / half
    damping = 1.0 / ratio
    pairs = [(0.0, 1.0 / centre)]
    for _ in range(CHEB - 1):
        following = 1.0 / (2.0 * ratio - damping)
        pairs.append((following * damping, 2.0 * following / half))
        damping = following
    return pairs


def split_pair(matrix):
    high = matrix.astype(ml_dtypes.bfloat16)
    low = (matrix - high.astype(np.float64)).astype(ml_dtypes.bfloat16)
    return high, low


def left_table(matrix):
    high, low = split_pair(matrix)
    return np.block([[high, high], [low, np.zeros_like(low)]])


def right_table(matrix):
    high, low = split_pair(matrix)
    return np.block([[high, low], [high, np.zeros_like(low)]])


def matrix_tables():
    weights, derive, stiff = quadrature_tables()
    scaled = stiff / weights[:, None]
    eye_y = np.eye(LY // 8)
    eye_z = np.eye(LZ // 8)
    lap_xy = np.kron(scaled, np.eye(LY)) + np.kron(np.eye(8), np.kron(eye_y, scaled))
    lap_z = np.kron(eye_z, scaled).T
    div_xy = np.concatenate(
        [np.kron(derive, np.eye(LY)), np.kron(np.eye(8), np.kron(eye_y, derive))], axis=1
    )
    div_z = np.kron(eye_z, derive).T
    return np.stack(
        [
            left_table(lap_xy),
            right_table(lap_z),
            np.concatenate(split_pair(div_xy), axis=0),
            right_table(div_z),
        ]
    )


def field_tables():
    weights, _, stiff = quadrature_tables()
    mass = weights[:, None, None] * np.tile(weights, 2)[None, :, None] * np.tile(weights, 16)
    shared = np.where(np.arange(8) % 7 == 0, 0.5, 1.0)
    shared_z = np.tile(shared, 16)
    shared_z[0] = shared_z[-1] = 1.0
    part = shared[:, None, None] * np.tile(shared, 2)[None, :, None] * shared_z

    def periodic(line):
        line = line.copy()
        line[0] = line[7] = line[0] + line[7]
        return line

    def column(line):
        line = np.tile(line, 16)
        total = line.copy()
        total[8::8] += line[7:-1:8]
        total[7:-1:8] += line[8::8]
        return total

    entry = np.diag(stiff)
    wx, sx = periodic(weights), periodic(entry)
    wy, sy = np.tile(wx, 2), np.tile(sx, 2)
    wz, sz = column(weights), column(entry)

    def outer(a, b, c):
        return a[:, None, None] * b[None, :, None] * c

    diagonal = outer(sx, wy, wz) + outer(wx, sy, wz) + outer(wx, wy, sz)
    diagonal = diagonal + SIGMA_SHIFT * outer(wx, wy, wz)
    return np.stack([mass / HALF, part, HALF / diagonal]).astype(np.float32)


def reduction_stages(nx, ny):
    bits_y = ny.bit_length() - 1
    bits = list(range(bits_y + nx.bit_length() - 1))
    first = [b for b in bits if b == 1 or b >= bits_y]
    stages = [first, [b for b in bits if b not in first]]
    return [stage for stage in stages if stage]


def step_kernel(nx, ny, *refs):
    (old_hbm, inv_hbm, bnd_hbm, mat_hbm, tab_hbm, fields, prs) = refs[:7]
    (old, inv, bnd, mat_ref, tab_ref, free, minv, basis, rem, upd) = refs[7:17]
    (vsnd, vrcv, vcsnd, vcrcv, psnd, prcv, pcsnd, pcrcv) = refs[17:25]
    (ssnd, srcv, scsnd, scrcv, hsum, hcsum, macc, arow, arcv) = refs[25:34]
    (lsem, vsem, psem, ssem, ass, ars) = refs[34:]

    gx = lax.axis_index("gx")
    gy = lax.axis_index("gy")

    def neighbour(dx, dy):
        return (lax.rem(gx + dx + nx, nx), lax.rem(gy + dy + ny, ny))

    me = gx * ny + gy
    bits_y = ny.bit_length() - 1

    def hops(b):
        if b < 2:
            return 2 * b
        return 1 << (b - 2) if b < bits_y else max(1, b - bits_y)

    stages = []
    for bits in reduction_stages(nx, ny):
        partners = []
        masks = range(1, 1 << len(bits))
        masks = sorted(masks, key=lambda m: -sum(hops(b) for i, b in enumerate(bits) if m >> i & 1))
        for mask in masks:
            other = me
            for place, b in enumerate(bits):
                if mask >> place & 1:
                    other = other + (1 - 2 * lax.rem(lax.div(me, 1 << b), 2)) * (1 << b)
            partners.append((mask, (lax.div(other, ny), lax.rem(other, ny))))
        stages.append(partners)

    barrier = pltpu.get_barrier_semaphore()
    greeted = 0
    for dx, dy, *_ in CORNERS + Y_FACES + X_FACES:
        pl.semaphore_signal(barrier, inc=1, device_id=neighbour(dx, dy), device_id_type=MESH)
        greeted += 1
    for partners in stages:
        for _, device in partners:
            pl.semaphore_signal(barrier, inc=1, device_id=device, device_id_type=MESH)
            greeted += 1

    loads = [
        pltpu.make_async_copy(inv_hbm, inv, lsem.at[0]),
        pltpu.make_async_copy(bnd_hbm, bnd, lsem.at[1]),
        pltpu.make_async_copy(tab_hbm, tab_ref, lsem.at[2]),
        pltpu.make_async_copy(old_hbm, old, lsem.at[3]),
        pltpu.make_async_copy(mat_hbm, mat_ref, lsem.at[4]),
    ]
    for load in loads:
        load.start()

    lane = lax.broadcasted_iota(jnp.int32, (128, 128), 1)
    z_first = (lax.rem(lane, 8) == 0) & (lane > 0)
    z_last = (lax.rem(lane, 8) == 7) & (lane < LZ - 1)
    row3 = lax.broadcasted_iota(jnp.int32, (8, 8, 128), 1)
    row3_first, row3_last = row3 == 0, row3 == 7
    row = lax.broadcasted_iota(jnp.int32, (8, 128), 0)
    row_first, row_last = row == 0, row == 7
    tile_lane = lax.broadcasted_iota(jnp.int32, (8, 128), 1)

    def planes(e):
        return pl.ds(8 * e, 8)

    def inner_sums(w):
        flat = w.reshape(128, 128)
        flat = (
            flat
            + jnp.where(z_first, pltpu.roll(flat, 1, 1), 0.0)
            + jnp.where(z_last, pltpu.roll(flat, 127, 1), 0.0)
        )
        w = flat.reshape(8, LY, 128)
        a, b = w[:, :8], w[:, 8:]
        a_sum = a + jnp.where(row3_last, pltpu.roll(b, 7, 1), 0.0)
        b_sum = b + jnp.where(row3_first, pltpu.roll(a, 1, 1), 0.0)
        return jnp.concatenate([a_sum, b_sum], axis=1)

    def assembled(local, emit, ends=None, done=None, gate=None):
        if gate is not None:
            w1, w2 = [inner_sums(w) for w in local((1, 2))]
            gate()
        w0, w3 = [inner_sums(w) for w in local((0, 3))]
        if ends is not None:
            ends(w0, w3)
        if gate is None:
            w1, w2 = [inner_sums(w) for w in local((1, 2))]
        both = w0[7:] + w1[:1]
        emit(0, jnp.concatenate([w0[:7], both], axis=0))
        w1 = jnp.concatenate([both, w1[1:]], axis=0)
        both = w1[7:] + w2[:1]
        emit(1, jnp.concatenate([w1[:7], both], axis=0))
        w2 = jnp.concatenate([both, w2[1:]], axis=0)
        both = w2[7:] + w3[:1]
        emit(2, jnp.concatenate([w2[:7], both], axis=0))
        emit(3, jnp.concatenate([both, w3[1:]], axis=0))
        if done is not None:
            done()

    class Faces:
        def __init__(self, send, receive, corner_send, corner_receive, sems):
            self.send, self.receive = send, receive
            self.corner_send, self.corner_receive = corner_send, corner_receive
            self.sems = sems

        def start(self, source, target, dx, dy, k):
            pltpu.make_async_remote_copy(
                src_ref=source,
                dst_ref=target,
                send_sem=self.sems(k),
                recv_sem=self.sems(k + 1),
                device_id=neighbour(dx, dy),
                device_id_type=MESH,
            ).start()

        def post(self, faces):
            for dx, dy, here, there, rows in faces:
                here, there = pl.ds(here, rows), pl.ds(there, rows)
                if len(self.send.shape) == 3:
                    source, target = self.send.at[:, here], self.receive.at[:, there]
                else:
                    source, target = self.send.at[here], self.receive.at[there]
                self.start(source, target, dx, dy, 0)

        def post_corners(self):
            for dx, dy, here, there in CORNERS:
                if len(self.send.shape) == 3:
                    source, target = self.corner_send.at[:, here], self.corner_receive.at[:, there]
                else:
                    source, target = self.corner_send.at[here], self.corner_receive.at[there]
                self.start(source, target, dx, dy, 2)

        def field(self, c):
            return Faces(
                self.send.at[c],
                self.receive.at[c],
                self.corner_send.at[c],
                self.corner_receive.at[c],
                self.sems,
            )

        def keep_corners(self, w0, w3):
            self.corner_send[0] = w0[0, :1]
            self.corner_send[1] = w0[0, LY - 1 :]
            self.corner_send[2] = w3[7, :1]
            self.corner_send[3] = w3[7, LY - 1 :]

        def keep_sides(self, w0, w3):
            self.send[pl.ds(0, 16), :] = w0[0]
            self.send[pl.ds(16, 16), :] = w3[7]

        def keep_ends(self, w0, w3):
            self.keep_corners(w0, w3)
            self.keep_sides(w0, w3)

        def ends(self, w0, w3):
            self.keep_corners(w0, w3)
            self.post_corners()
            self.keep_sides(w0, w3)
            self.post(X_FACES)

        def rows(self, e, w):
            self.send[pl.ds(32 + 8 * e, 8), :] = w[:, 0, :]
            self.send[pl.ds(64 + 8 * e, 8), :] = w[:, LY - 1, :]

        def done(self):
            self.post(Y_FACES)

        def post_all(self):
            self.post_corners()
            self.post(Y_FACES + X_FACES)

        def arrived(self):
            wait_all(self.receive, self.sems(1))
            wait_all(self.corner_receive, self.sems(3))

        def faces_arrived(self):
            wait_all(self.receive, self.sems(1))

        def corners_arrived(self):
            wait_all(self.corner_receive, self.sems(3))

        def sent(self):
            wait_all(self.send, self.sems(0))
            wait_all(self.corner_send, self.sems(2))

    def velocity_faces(slot, c):
        return Faces(
            vsnd.at[slot, c],
            vrcv.at[slot, c],
            vcsnd.at[slot, c],
            vcrcv.at[slot, c],
            lambda k: vsem.at[k, slot, c],
        )

    def pressure_faces(slot):
        return Faces(
            psnd.at[slot],
            prcv.at[slot],
            pcsnd.at[slot],
            pcrcv.at[slot],
            lambda k: psem.at[k, slot],
        )

    def source_faces(j):
        return Faces(
            ssnd.at[j], srcv.at[j], scsnd.at[j], scrcv.at[j], lambda k: ssem.at[k, j]
        )

    def spread_row(line):
        return jnp.broadcast_to(line, (8, 128))

    def halo(faces, corners, e):
        out = []
        for x in range(8):
            first = spread_row(faces[pl.ds(32 + 8 * e + x, 1), :])
            last = spread_row(faces[pl.ds(64 + 8 * e + x, 1), :])
            side = None
            if e == 0 and x == 0:
                side, corner = 0, 0
            if e == ELEMENTS - 1 and x == 7:
                side, corner = 16, 2
            if side is not None:
                first = first + spread_row(corners[corner])
                last = last + spread_row(corners[corner + 1])
            first = jnp.where(row_first, first, 0.0)
            last = jnp.where(row_last, last, 0.0)
            if side is not None:
                first = first + faces[pl.ds(side, 8), :]
                last = last + faces[pl.ds(side + 8, 8), :]
            out.append(jnp.concatenate([first, last], axis=0))
        return jnp.stack(out)

    def wait_all(ref, sem):
        pltpu.make_async_copy(ref, ref, sem).wait()

    def halves(v):
        high = v.astype(jnp.bfloat16)
        return high, (v - high.astype(F32)).astype(jnp.bfloat16)

    def along_z(highs, lows, index):
        rows = [jnp.concatenate([h, l], axis=1) for h, l in zip(highs, lows)]
        out = jnp.dot(
            jnp.concatenate(rows, axis=0), mat_ref[index], preferred_element_type=F32
        )
        out = out[:, :128] + out[:, 128:]
        return [out[:128], out[128:]]

    def split_blocks(blocks):
        pairs = [halves(v.reshape(128, 128)) for v in blocks]
        return [p[0] for p in pairs], [p[1] for p in pairs]

    def laplace(blocks):
        highs, lows = split_blocks(blocks)
        stacked = jnp.concatenate(
            [jnp.concatenate(highs, axis=1), jnp.concatenate(lows, axis=1)], axis=0
        )
        xy = jnp.dot(mat_ref[0], stacked, preferred_element_type=F32)
        xy = xy[:128] + xy[128:]
        z = along_z(highs, lows, 1)
        return [
            (xy[:, :128] + z[0]).reshape(8, LY, 128),
            (xy[:, 128:] + z[1]).reshape(8, LY, 128),
        ]

    mass, part, invd = tab_ref.at[0], tab_ref.at[1], tab_ref.at[2]

    def tile_sum(a):
        a = a.reshape(16, 8, 128)
        total = a[0]
        for k in range(1, 16):
            total = total + a[k]
        return total

    def record(slot, total):
        lanes = jnp.sum(total, axis=1, keepdims=True)
        macc[...] += jnp.where(tile_lane == slot, lanes, 0.0)

    for load in loads[:3]:
        load.wait()
    macc[...] = jnp.zeros_like(macc)
    for e in range(ELEMENTS):
        free[planes(e)] = bnd[planes(e)].astype(F32)
        scaled = mass[...] * inv[planes(e)]
        minv[0, planes(e)] = scaled
        minv[1, planes(e)] = scaled * (1.0 / THERMAL)
        for c in range(4):
            basis[0, c, planes(e)] = jnp.zeros((8, LY, 128), F32)
    loads[3].wait()

    for c in range(4):

        def local_right(e, c=c):
            value = minv[0, planes(e)] * old[c, planes(e)]
            if c == 2:
                value = value + mass[...] * (COUPLING * old[3, planes(e)])
            if c == 3:
                value = value - mass[...] * (STRATIFY * old[2, planes(e)])
            return value

        faces = velocity_faces(0, c)

        def emit_right(e, w, c=c, faces=faces):
            basis[1, c, planes(e)] = free[planes(e)] * w
            faces.rows(e, w)

        def ends_right(w0, w3, c=c, faces=faces):
            if c == 0:
                pl.semaphore_wait(barrier, greeted)
            faces.ends(w0, w3)

        assembled(lambda es, f=local_right: [f(e) for e in es], emit_right, ends_right, faces.done)
    loads[4].wait()

    shift = CENTRE / HALF

    def divergence(c, blocks):
        highs, lows = split_blocks(blocks)
        if c == 2:
            out = along_z(highs, lows, 3)
        else:
            table = mat_ref[2, :, pl.ds(128 * c, 128)]
            high = jnp.dot(table, jnp.concatenate(highs, axis=1), preferred_element_type=F32)
            low = jnp.dot(
                table[:128], jnp.concatenate(lows, axis=1), preferred_element_type=F32
            )
            total = high[:128] + high[128:] + low
            out = [total[:, :128], total[:, 128:]]
        return [block.reshape(8, LY, 128) for block in out]

    pairs = chebyshev_coefficients()

    def operator(updates):
        laps = laplace(updates)
        return [mass[...] * (lap + SIGMA_SHIFT * u) for lap, u in zip(laps, updates)]

    def source_parts(j):
        group = source_faces(j)
        for c in range(3):
            faces = group.field(c)

            def local(es, c=c):
                blocks = [basis[j + 1, c, planes(e)] for e in es]
                return [mass[...] * out for out in divergence(c, blocks)]

            assembled(local, faces.rows, faces.keep_ends)
        group.post_all()

    def krylov(j, last):
        now = lax.rem(j, 2)
        later = 1 - now
        for c in range(4):
            here = velocity_faces(now, c)
            there = velocity_faces(later, c)
            gate = here.corners_arrived if c == 0 and not last else None
            if gate is None:
                here.arrived()
            else:
                here.faces_arrived()
            totals = [jnp.zeros((8, 128), F32)] * 3
            if not last:

                @pl.when(j >= 1)
                def _(there=there):
                    there.sent()

            def local(es, c=c, totals=totals, here=here):
                blocks = []
                for e in es:
                    v = basis[j + 1, c, planes(e)] + free[planes(e)] * halo(
                        here.receive, here.corner_receive, e
                    )
                    basis[j + 1, c, planes(e)] = v
                    weighted = v * part[...]
                    totals[0] = totals[0] + tile_sum(weighted * v)
                    totals[1] = totals[1] + tile_sum(weighted * basis[j, c, planes(e)])
                    blocks.append(v)
                out = []
                for e, v, lap in zip(es, blocks, laplace(blocks)):
                    w = mass[...] * lap + minv[c // 3, planes(e)] * v
                    if last:
                        totals[2] = totals[2] + tile_sum(w * v)
                    out.append(w)
                return out

            def emit(e, w, c=c, there=there):
                basis[j + 2, c, planes(e)] = (
                    free[planes(e)] * w
                    - shift * basis[j + 1, c, planes(e)]
                    - basis[j, c, planes(e)]
                )
                there.rows(e, w)

            if last:
                for es in ((0, 3), (1, 2)):
                    local(es)
            else:
                assembled(local, emit, there.ends, there.done, gate)
            record(4 * j + c, totals[0])
            record(4 * (ITERS + j) + c, totals[1])
            if last:
                record(4 * 2 * ITERS + c, totals[2])

    def krylov_body(j, carry):
        krylov(j, False)

        source_parts(j)
        return carry

    lax.fori_loop(0, ITERS - 1, krylov_body, 0)
    krylov(jnp.int32(ITERS - 1), True)

    value = jnp.sum(macc[...], axis=0, keepdims=True)
    posted = []
    for k, partners in enumerate(stages):
        arow[k] = value
        copies = []
        for mask, device in partners:
            copy = pltpu.make_async_remote_copy(
                src_ref=arow.at[k],
                dst_ref=arcv.at[k, mask],
                send_sem=ass.at[k, mask],
                recv_sem=ars.at[k, mask],
                device_id=device,
                device_id_type=MESH,
            )
            copy.start()
            copies.append(copy)
        if k == 0:
            source_parts(jnp.int32(ITERS - 1))
        for (mask, _), copy in zip(partners, copies):
            copy.wait_recv()
        for mask, _ in partners:
            value = value + arcv[k, mask]
        posted.extend(copies)

    def moment(index):
        return value if index == 0 else pltpu.roll(value, 128 - 4 * index, 1)

    q = [moment(j) for j in range(ITERS)]
    r = [moment(ITERS + j) for j in range(1, ITERS)]
    r.append(moment(2 * ITERS) - shift * q[-1] - r[-1])
    nu = []
    for j in range(ITERS):
        nu.append(q[j] - q[j - 1] if j else q[0])
        nu.append(r[j] - r[j - 1] if j else r[0])

    def gram(i, j):
        total = None
        for k in range(min(i, j) + 1):
            term = nu[abs(i - j) + 2 * k]
            total = term if total is None else total + term
        return total

    system = [[None] * ITERS for _ in range(ITERS)]
    for i in range(ITERS):
        for j in range(i, ITERS):
            entry = shift * gram(i, j) + gram(i, j + 1)
            if j:
                entry = entry + gram(i, j - 1)
            system[i][j] = entry
    right = [nu[i] for i in range(ITERS)]
    inverse = []
    for k in range(ITERS):
        inverse.append(1.0 / system[k][k])
        for i in range(k + 1, ITERS):
            factor = system[k][i] * inverse[k]
            for j in range(i, ITERS):
                system[i][j] = system[i][j] - factor * system[k][j]
            right[i] = right[i] - factor * right[k]
    answer = [None] * ITERS
    for k in reversed(range(ITERS)):
        total = right[k]
        for j in range(k + 1, ITERS):
            total = total - system[k][j] * answer[j]
        answer[k] = total * inverse[k]

    lane_row = lax.broadcasted_iota(jnp.int32, (1, 128), 1)

    def coefficients(c):
        out = []
        for j in range(ITERS):
            one = jnp.sum(jnp.where(lane_row == c, answer[j], 0.0), axis=1, keepdims=True)
            if c == 3:
                one = one * (1.0 / THERMAL)
            out.append(jnp.broadcast_to(one, (8, 128)).reshape(1, 8, 128))
        return out

    def combine(c, weights):
        for x in range(0, LX, 8):
            for y in range(0, LY, 8):
                where = (pl.ds(x, 8), pl.ds(y, 8))
                total = weights[0] * basis[1, c, where[0], where[1]]
                for j in range(1, ITERS):
                    total = total + weights[j] * basis[j + 1, c, where[0], where[1]]
                fields[c, where[0], where[1]] = total

    known = [coefficients(c) for c in range(3)]
    for c in range(3):
        combine(c, known[c])

    for j in range(ITERS):
        source_faces(j).arrived()
    for r in range(0, FACE_ROWS, 8):
        total = None
        for c in range(3):
            for j in range(ITERS):
                term = known[c][j][0] * srcv[j, c, pl.ds(r, 8), :]
                total = term if total is None else total + term
        hsum[pl.ds(r, 8), :] = total
    for k in range(4):
        total = None
        for c in range(3):
            for j in range(ITERS):
                term = known[c][j][0, :1] * scrcv[j, c, k]
                total = term if total is None else total + term
        hcsum[k] = total

    def local_source(es):
        totals = None
        for c in range(3):
            terms = divergence(c, [fields[c, planes(e)] for e in es])
            totals = terms if totals is None else [a + b for a, b in zip(totals, terms)]
        return [mass[...] * total for total in totals]

    def emit_source(e, w):
        left = -free[planes(e)] * (w + halo(hsum, hcsum, e))
        update = pairs[0][1] * (invd[...] * left)
        rem[planes(e)] = left
        upd[planes(e)] = update
        prs[planes(e)] = update

    def apply_pressure(local, faces):
        def emit(e, w):
            rem[planes(e)] = rem[planes(e)] - free[planes(e)] * w
            faces.rows(e, w)

        assembled(local, emit, faces.ends, faces.done)

    assembled(local_source, emit_source)
    apply_pressure(lambda es: operator([upd[planes(e)] for e in es]), pressure_faces(0))
    combine(3, coefficients(3))

    def refreshed(e, faces, keep, gain):
        left = rem[planes(e)] - free[planes(e)] * halo(faces.receive, faces.corner_receive, e)
        update = keep * upd[planes(e)] + gain * (invd[...] * left)
        prs[planes(e)] = prs[planes(e)] + update
        return left, update

    def chebyshev_body(i, carry):
        now = lax.rem(i + 1, 2)
        here = pressure_faces(now)
        there = pressure_faces(1 - now)
        keep, gain = jnp.float32(pairs[1][0]), jnp.float32(pairs[1][1])
        for k in range(2, CHEB - 1):
            keep = jnp.where(i == k, jnp.float32(pairs[k][0]), keep)
            gain = jnp.where(i == k, jnp.float32(pairs[k][1]), gain)

        here.arrived()

        @pl.when(i >= 2)
        def _():
            there.sent()

        def local(es):
            updates = []
            for e in es:
                left, update = refreshed(e, here, keep, gain)
                rem[planes(e)] = left
                upd[planes(e)] = update
                updates.append(update)
            return operator(updates)

        apply_pressure(local, there)
        return carry

    lax.fori_loop(1, CHEB - 1, chebyshev_body, 0)
    here = pressure_faces(CHEB % 2)
    here.arrived()
    for e in range(ELEMENTS):
        refreshed(e, here, pairs[CHEB - 1][0], pairs[CHEB - 1][1])
    for copy in posted:
        copy.wait_send()
    for slot in range(2):
        pressure_faces(slot).sent()
        for c in range(4):
            velocity_faces(slot, c).sent()
    for j in range(ITERS):
        source_faces(j).sent()


def store_kernel(fields, pressure, new_hbm, prs_hbm, sems):
    stores = [
        pltpu.make_async_copy(fields, new_hbm, sems.at[0]),
        pltpu.make_async_copy(pressure, prs_hbm, sems.at[1]),
    ]
    for store in stores:
        store.start()
    for store in stores:
        store.wait()


def solution(mesh):
    nx, ny = mesh.shape["gx"], mesh.shape["gy"]
    stages = reduction_stages(nx, ny)
    most = max(1 << len(bits) for bits in stages)
    matrices = matrix_tables()
    tables = field_tables()
    brick = (LX, LY, LZ)

    def body(*refs):
        step_kernel(nx, ny, *refs)

    def on_device(old_fields, inverse_step, boundary):
        any_space = pl.BlockSpec(memory_space=pl.ANY)
        operands = (old_fields, inverse_step, boundary, jnp.asarray(matrices), jnp.asarray(tables))
        operands = [pltpu.with_memory_space_constraint(x, pltpu.HBM) for x in operands]
        results = pl.pallas_call(
            body,
            out_shape=(pltpu.VMEM((4,) + brick, F32), pltpu.VMEM(brick, F32)),
            in_specs=[any_space] * 5,
            out_specs=(pl.BlockSpec(memory_space=pltpu.VMEM),) * 2,
            scratch_shapes=[
                pltpu.VMEM((4,) + brick, F32),
                pltpu.VMEM(brick, F32),
                pltpu.VMEM(brick, jnp.int32),
                pltpu.VMEM(matrices.shape, jnp.bfloat16),
                pltpu.VMEM(tables.shape, F32),
                pltpu.VMEM(brick, F32),
                pltpu.VMEM((2,) + brick, F32),
                pltpu.VMEM((ITERS + 1, 4) + brick, F32),
                pltpu.VMEM(brick, F32),
                pltpu.VMEM(brick, F32),
                pltpu.VMEM((2, 4, FACE_ROWS, 128), F32),
                pltpu.VMEM((2, 4, FACE_ROWS, 128), F32),
                pltpu.VMEM((2, 4, 4, 1, 128), F32),
                pltpu.VMEM((2, 4, 4, 1, 128), F32),
                pltpu.VMEM((2, FACE_ROWS, 128), F32),
                pltpu.VMEM((2, FACE_ROWS, 128), F32),
                pltpu.VMEM((2, 4, 1, 128), F32),
                pltpu.VMEM((2, 4, 1, 128), F32),
                pltpu.VMEM((ITERS, 3, FACE_ROWS, 128), F32),
                pltpu.VMEM((ITERS, 3, FACE_ROWS, 128), F32),
                pltpu.VMEM((ITERS, 3, 4, 1, 128), F32),
                pltpu.VMEM((ITERS, 3, 4, 1, 128), F32),
                pltpu.VMEM((FACE_ROWS, 128), F32),
                pltpu.VMEM((4, 1, 128), F32),
                pltpu.VMEM((8, 128), F32),
                pltpu.VMEM((len(stages), 1, 128), F32),
                pltpu.VMEM((len(stages), most, 1, 128), F32),
                pltpu.SemaphoreType.DMA((5,)),
                pltpu.SemaphoreType.DMA((4, 2, 4)),
                pltpu.SemaphoreType.DMA((4, 2)),
                pltpu.SemaphoreType.DMA((4, ITERS)),
                pltpu.SemaphoreType.DMA((len(stages), most)),
                pltpu.SemaphoreType.DMA((len(stages), most)),
            ],
            compiler_params=pltpu.CompilerParams(
                collective_id=0, has_side_effects=True, vmem_limit_bytes=40 * 1024 * 1024
            ),
        )(*operands)
        results = [pltpu.with_memory_space_constraint(x, pltpu.VMEM) for x in results]
        return pl.pallas_call(
            store_kernel,
            out_shape=(
                jax.ShapeDtypeStruct((4,) + brick, F32),
                jax.ShapeDtypeStruct(brick, F32),
            ),
            in_specs=[any_space] * 2,
            out_specs=(any_space, any_space),
            scratch_shapes=[pltpu.SemaphoreType.DMA((2,))],
            compiler_params=pltpu.CompilerParams(vmem_limit_bytes=8 * 1024 * 1024),
        )(*results)

    return jax.shard_map(
        on_device,
        mesh=mesh,
        in_specs=(P(None, "gx", "gy", None), P("gx", "gy", None), P("gx", "gy", None)),
        out_specs=(P(None, "gx", "gy", None), P("gx", "gy", None)),
        check_vma=False,
    )
```

```python
import jax
import jax.numpy as jnp
import ml_dtypes
import numpy as np
from jax import lax
from jax.experimental import pallas as pl
from jax.experimental.pallas import tpu as pltpu
from jax.sharding import PartitionSpec as P

ITERS = 6
CHEB = 6
SIGMA_SHIFT = 0.5
THERMAL = 1.4
COUPLING = 1.0
STRATIFY = 1.0
SPREAD = 20.0
CENTRE = 6.0
HALF = 2.9
LOBATTO_POINTS = (
    -1.0,
    -0.8717401485096066,
    -0.5917001814331423,
    -0.2092992179024789,
    0.2092992179024789,
    0.5917001814331423,
    0.8717401485096066,
    1.0,
)
MESH = pl.DeviceIdType.MESH
LX, LY, LZ = 32, 16, 128
ELEMENTS = LX // 8
F32 = jnp.float32
X_FACES = ((-1, 0, 0, 16, 16), (1, 0, 16, 0, 16))
Y_FACES = ((0, -1, 32, 64, 32), (0, 1, 64, 32, 32))
FACE_ROWS = 96
CORNERS = ((-1, -1, 0, 3), (-1, 1, 1, 2), (1, -1, 2, 1), (1, 1, 3, 0))


def legendre_value(points, degree):
    previous = points * 0.0 + 1.0
    current = points
    for order in range(1, degree):
        following = ((2 * order + 1) * points * current - order * previous) / (order + 1)
        previous = current
        current = following
    return current


def quadrature_tables():
    degree = 7
    points = np.array(LOBATTO_POINTS)
    values = legendre_value(points, degree)
    weights = 2.0 / (degree * (degree + 1) * values * values)
    derive = np.zeros((degree + 1, degree + 1))
    for row in range(degree + 1):
        for column in range(degree + 1):
            if row != column:
                derive[row, column] = values[row] / (
                    values[column] * (points[row] - points[column])
                )
    derive[0, 0] = -degree * (degree + 1) / 4.0
    derive[degree, degree] = degree * (degree + 1) / 4.0
    return weights, derive, derive.T @ (weights[:, None] * derive)


def chebyshev_bounds():
    weights, _, stiff = quadrature_tables()
    w = np.diag(weights)
    element = np.kron(np.kron(stiff, w), w)
    element = element + np.kron(np.kron(w, stiff), w)
    element = element + np.kron(np.kron(w, w), stiff)
    element = element + SIGMA_SHIFT * np.kron(np.kron(w, w), w)
    upper = float(np.max(np.sum(np.abs(element), axis=1) / np.diag(element)))
    lower = upper / SPREAD
    return (upper + lower) / 2.0, (upper - lower) / 2.0


def chebyshev_coefficients():
    centre, half = chebyshev_bounds()
    ratio = centre / half
    damping = 1.0 / ratio
    pairs = [(0.0, 1.0 / centre)]
    for _ in range(CHEB - 1):
        following = 1.0 / (2.0 * ratio - damping)
        pairs.append((following * damping, 2.0 * following / half))
        damping = following
    return pairs


def split_pair(matrix):
    high = matrix.astype(ml_dtypes.bfloat16)
    low = (matrix - high.astype(np.float64)).astype(ml_dtypes.bfloat16)
    return high, low


def left_table(matrix):
    high, low = split_pair(matrix)
    return np.block([[high, high], [low, np.zeros_like(low)]])


def right_table(matrix):
    high, low = split_pair(matrix)
    return np.block([[high, low], [high, np.zeros_like(low)]])


def matrix_tables():
    weights, derive, stiff = quadrature_tables()
    scaled = stiff / weights[:, None]
    eye_y = np.eye(LY // 8)
    eye_z = np.eye(LZ // 8)
    lap_xy = np.kron(scaled, np.eye(LY)) + np.kron(np.eye(8), np.kron(eye_y, scaled))
    lap_z = np.kron(eye_z, scaled).T
    div_xy = np.concatenate(
        [np.kron(derive, np.eye(LY)), np.kron(np.eye(8), np.kron(eye_y, derive))], axis=1
    )
    div_z = np.kron(eye_z, derive).T
    return np.stack(
        [
            left_table(lap_xy),
            right_table(lap_z),
            np.concatenate(split_pair(div_xy), axis=0),
            right_table(div_z),
        ]
    )


def field_tables():
    weights, _, stiff = quadrature_tables()
    mass = weights[:, None, None] * np.tile(weights, 2)[None, :, None] * np.tile(weights, 16)
    shared = np.where(np.arange(8) % 7 == 0, 0.5, 1.0)
    shared_z = np.tile(shared, 16)
    shared_z[0] = shared_z[-1] = 1.0
    part = shared[:, None, None] * np.tile(shared, 2)[None, :, None] * shared_z

    def periodic(line):
        line = line.copy()
        line[0] = line[7] = line[0] + line[7]
        return line

    def column(line):
        line = np.tile(line, 16)
        total = line.copy()
        total[8::8] += line[7:-1:8]
        total[7:-1:8] += line[8::8]
        return total

    entry = np.diag(stiff)
    wx, sx = periodic(weights), periodic(entry)
    wy, sy = np.tile(wx, 2), np.tile(sx, 2)
    wz, sz = column(weights), column(entry)

    def outer(a, b, c):
        return a[:, None, None] * b[None, :, None] * c

    diagonal = outer(sx, wy, wz) + outer(wx, sy, wz) + outer(wx, wy, sz)
    diagonal = diagonal + SIGMA_SHIFT * outer(wx, wy, wz)
    return np.stack([mass / HALF, part, HALF / diagonal]).astype(np.float32)


def reduction_stages(nx, ny):
    bits_y = ny.bit_length() - 1
    bits = list(range(bits_y + nx.bit_length() - 1))
    first = [b for b in bits if b == 1 or b >= bits_y]
    stages = [first, [b for b in bits if b not in first]]
    return [stage for stage in stages if stage]


def step_kernel(nx, ny, *refs):
    (old_hbm, inv_hbm, bnd_hbm, mat_hbm, tab_hbm, fields, prs) = refs[:7]
    (old, inv, bnd, mat_ref, tab_ref, free, minv, basis, parts, rem, upd) = refs[7:18]
    (vsnd, vrcv, vcsnd, vcrcv, psnd, prcv, pcsnd, pcrcv) = refs[18:26]
    (ssnd, srcv, scsnd, scrcv, hsum, hcsum, macc, arow, arcv) = refs[26:35]
    (lsem, vsem, psem, ssem, ass, ars) = refs[35:]

    gx = lax.axis_index("gx")
    gy = lax.axis_index("gy")

    def neighbour(dx, dy):
        return (lax.rem(gx + dx + nx, nx), lax.rem(gy + dy + ny, ny))

    me = gx * ny + gy
    bits_y = ny.bit_length() - 1

    def hops(b):
        if b < 2:
            return 2 * b
        return 1 << (b - 2) if b < bits_y else max(1, b - bits_y)

    stages = []
    for bits in reduction_stages(nx, ny):
        partners = []
        masks = range(1, 1 << len(bits))
        masks = sorted(masks, key=lambda m: -sum(hops(b) for i, b in enumerate(bits) if m >> i & 1))
        for mask in masks:
            other = me
            for place, b in enumerate(bits):
                if mask >> place & 1:
                    other = other + (1 - 2 * lax.rem(lax.div(me, 1 << b), 2)) * (1 << b)
            partners.append((mask, (lax.div(other, ny), lax.rem(other, ny))))
        stages.append(partners)

    barrier = pltpu.get_barrier_semaphore()
    greeted = 0
    for dx, dy, *_ in CORNERS + Y_FACES + X_FACES:
        pl.semaphore_signal(barrier, inc=1, device_id=neighbour(dx, dy), device_id_type=MESH)
        greeted += 1
    for partners in stages:
        for _, device in partners:
            pl.semaphore_signal(barrier, inc=1, device_id=device, device_id_type=MESH)
            greeted += 1

    loads = [
        pltpu.make_async_copy(inv_hbm, inv, lsem.at[0]),
        pltpu.make_async_copy(bnd_hbm, bnd, lsem.at[1]),
        pltpu.make_async_copy(tab_hbm, tab_ref, lsem.at[2]),
        pltpu.make_async_copy(old_hbm, old, lsem.at[3]),
        pltpu.make_async_copy(mat_hbm, mat_ref, lsem.at[4]),
    ]
    for load in loads:
        load.start()

    lane = lax.broadcasted_iota(jnp.int32, (128, 128), 1)
    z_first = (lax.rem(lane, 8) == 0) & (lane > 0)
    z_last = (lax.rem(lane, 8) == 7) & (lane < LZ - 1)
    row3 = lax.broadcasted_iota(jnp.int32, (8, 8, 128), 1)
    row3_first, row3_last = row3 == 0, row3 == 7
    row = lax.broadcasted_iota(jnp.int32, (8, 128), 0)
    row_first, row_last = row == 0, row == 7
    tile_lane = lax.broadcasted_iota(jnp.int32, (8, 128), 1)

    def planes(e):
        return pl.ds(8 * e, 8)

    def inner_sums(w):
        flat = w.reshape(128, 128)
        flat = (
            flat
            + jnp.where(z_first, pltpu.roll(flat, 1, 1), 0.0)
            + jnp.where(z_last, pltpu.roll(flat, 127, 1), 0.0)
        )
        w = flat.reshape(8, LY, 128)
        a, b = w[:, :8], w[:, 8:]
        a_sum = a + jnp.where(row3_last, pltpu.roll(b, 7, 1), 0.0)
        b_sum = b + jnp.where(row3_first, pltpu.roll(a, 1, 1), 0.0)
        return jnp.concatenate([a_sum, b_sum], axis=1)

    def assembled(local, emit, ends=None, done=None, gate=None):
        if gate is not None:
            w1, w2 = [inner_sums(w) for w in local((1, 2))]
            gate()
        w0, w3 = [inner_sums(w) for w in local((0, 3))]
        if ends is not None:
            ends(w0, w3)
        if gate is None:
            w1, w2 = [inner_sums(w) for w in local((1, 2))]
        both = w0[7:] + w1[:1]
        emit(0, jnp.concatenate([w0[:7], both], axis=0))
        w1 = jnp.concatenate([both, w1[1:]], axis=0)
        both = w1[7:] + w2[:1]
        emit(1, jnp.concatenate([w1[:7], both], axis=0))
        w2 = jnp.concatenate([both, w2[1:]], axis=0)
        both = w2[7:] + w3[:1]
        emit(2, jnp.concatenate([w2[:7], both], axis=0))
        emit(3, jnp.concatenate([both, w3[1:]], axis=0))
        if done is not None:
            done()

    class Faces:
        def __init__(self, send, receive, corner_send, corner_receive, sems):
            self.send, self.receive = send, receive
            self.corner_send, self.corner_receive = corner_send, corner_receive
            self.sems = sems

        def start(self, source, target, dx, dy, k):
            pltpu.make_async_remote_copy(
                src_ref=source,
                dst_ref=target,
                send_sem=self.sems(k),
                recv_sem=self.sems(k + 1),
                device_id=neighbour(dx, dy),
                device_id_type=MESH,
            ).start()

        def post(self, faces):
            for dx, dy, here, there, rows in faces:
                here, there = pl.ds(here, rows), pl.ds(there, rows)
                if len(self.send.shape) == 3:
                    source, target = self.send.at[:, here], self.receive.at[:, there]
                else:
                    source, target = self.send.at[here], self.receive.at[there]
                self.start(source, target, dx, dy, 0)

        def post_corners(self):
            for dx, dy, here, there in CORNERS:
                if len(self.send.shape) == 3:
                    source, target = self.corner_send.at[:, here], self.corner_receive.at[:, there]
                else:
                    source, target = self.corner_send.at[here], self.corner_receive.at[there]
                self.start(source, target, dx, dy, 2)

        def field(self, c):
            return Faces(
                self.send.at[c],
                self.receive.at[c],
                self.corner_send.at[c],
                self.corner_receive.at[c],
                self.sems,
            )

        def keep_corners(self, w0, w3):
            self.corner_send[0] = w0[0, :1]
            self.corner_send[1] = w0[0, LY - 1 :]
            self.corner_send[2] = w3[7, :1]
            self.corner_send[3] = w3[7, LY - 1 :]

        def keep_sides(self, w0, w3):
            self.send[pl.ds(0, 16), :] = w0[0]
            self.send[pl.ds(16, 16), :] = w3[7]

        def keep_ends(self, w0, w3):
            self.keep_corners(w0, w3)
            self.keep_sides(w0, w3)

        def ends(self, w0, w3):
            self.keep_corners(w0, w3)
            self.post_corners()
            self.keep_sides(w0, w3)
            self.post(X_FACES)

        def rows(self, e, w):
            self.send[pl.ds(32 + 8 * e, 8), :] = w[:, 0, :]
            self.send[pl.ds(64 + 8 * e, 8), :] = w[:, LY - 1, :]

        def done(self):
            self.post(Y_FACES)

        def post_all(self):
            self.post_corners()
            self.post(Y_FACES + X_FACES)

        def arrived(self):
            wait_all(self.receive, self.sems(1))
            wait_all(self.corner_receive, self.sems(3))

        def faces_arrived(self):
            wait_all(self.receive, self.sems(1))

        def corners_arrived(self):
            wait_all(self.corner_receive, self.sems(3))

        def sent(self):
            wait_all(self.send, self.sems(0))
            wait_all(self.corner_send, self.sems(2))

    def velocity_faces(slot, c):
        return Faces(
            vsnd.at[slot, c],
            vrcv.at[slot, c],
            vcsnd.at[slot, c],
            vcrcv.at[slot, c],
            lambda k: vsem.at[k, slot, c],
        )

    def pressure_faces(slot):
        return Faces(
            psnd.at[slot],
            prcv.at[slot],
            pcsnd.at[slot],
            pcrcv.at[slot],
            lambda k: psem.at[k, slot],
        )

    def source_faces(j):
        return Faces(
            ssnd.at[j], srcv.at[j], scsnd.at[j], scrcv.at[j], lambda k: ssem.at[k, j]
        )

    def spread_row(line):
        return jnp.broadcast_to(line, (8, 128))

    def halo(faces, corners, e):
        out = []
        for x in range(8):
            first = spread_row(faces[pl.ds(32 + 8 * e + x, 1), :])
            last = spread_row(faces[pl.ds(64 + 8 * e + x, 1), :])
            side = None
            if e == 0 and x == 0:
                side, corner = 0, 0
            if e == ELEMENTS - 1 and x == 7:
                side, corner = 16, 2
            if side is not None:
                first = first + spread_row(corners[corner])
                last = last + spread_row(corners[corner + 1])
            first = jnp.where(row_first, first, 0.0)
            last = jnp.where(row_last, last, 0.0)
            if side is not None:
                first = first + faces[pl.ds(side, 8), :]
                last = last + faces[pl.ds(side + 8, 8), :]
            out.append(jnp.concatenate([first, last], axis=0))
        return jnp.stack(out)

    def wait_all(ref, sem):
        pltpu.make_async_copy(ref, ref, sem).wait()

    def halves(v):
        high = v.astype(jnp.bfloat16)
        return high, (v - high.astype(F32)).astype(jnp.bfloat16)

    def along_z(highs, lows, index):
        rows = [jnp.concatenate([h, l], axis=1) for h, l in zip(highs, lows)]
        out = jnp.dot(
            jnp.concatenate(rows, axis=0), mat_ref[index], preferred_element_type=F32
        )
        out = out[:, :128] + out[:, 128:]
        return [out[:128], out[128:]]

    def split_blocks(blocks):
        pairs = [halves(v.reshape(128, 128)) for v in blocks]
        return [p[0] for p in pairs], [p[1] for p in pairs]

    def laplace(blocks):
        highs, lows = split_blocks(blocks)
        stacked = jnp.concatenate(
            [jnp.concatenate(highs, axis=1), jnp.concatenate(lows, axis=1)], axis=0
        )
        xy = jnp.dot(mat_ref[0], stacked, preferred_element_type=F32)
        xy = xy[:128] + xy[128:]
        z = along_z(highs, lows, 1)
        return [
            (xy[:, :128] + z[0]).reshape(8, LY, 128),
            (xy[:, 128:] + z[1]).reshape(8, LY, 128),
        ]

    mass, part, invd = tab_ref.at[0], tab_ref.at[1], tab_ref.at[2]

    def tile_sum(a):
        a = a.reshape(16, 8, 128)
        total = a[0]
        for k in range(1, 16):
            total = total + a[k]
        return total

    def record(slot, total):
        lanes = jnp.sum(total, axis=1, keepdims=True)
        macc[...] += jnp.where(tile_lane == slot, lanes, 0.0)

    for load in loads[:3]:
        load.wait()
    macc[...] = jnp.zeros_like(macc)
    for e in range(ELEMENTS):
        free[planes(e)] = bnd[planes(e)].astype(F32)
        scaled = mass[...] * inv[planes(e)]
        minv[0, planes(e)] = scaled
        minv[1, planes(e)] = scaled * (1.0 / THERMAL)
        for c in range(4):
            basis[0, c, planes(e)] = jnp.zeros((8, LY, 128), F32)
    loads[3].wait()

    for c in range(4):

        def local_right(e, c=c):
            value = minv[0, planes(e)] * old[c, planes(e)]
            if c == 2:
                value = value + mass[...] * (COUPLING * old[3, planes(e)])
            if c == 3:
                value = value - mass[...] * (STRATIFY * old[2, planes(e)])
            return value

        faces = velocity_faces(0, c)

        def emit_right(e, w, c=c, faces=faces):
            basis[1, c, planes(e)] = free[planes(e)] * w
            faces.rows(e, w)

        def ends_right(w0, w3, c=c, faces=faces):
            if c == 0:
                pl.semaphore_wait(barrier, greeted)
            faces.ends(w0, w3)

        assembled(lambda es, f=local_right: [f(e) for e in es], emit_right, ends_right, faces.done)
    loads[4].wait()

    shift = CENTRE / HALF

    def divergence(c, blocks):
        highs, lows = split_blocks(blocks)
        if c == 2:
            out = along_z(highs, lows, 3)
        else:
            table = mat_ref[2, :, pl.ds(128 * c, 128)]
            high = jnp.dot(table, jnp.concatenate(highs, axis=1), preferred_element_type=F32)
            low = jnp.dot(
                table[:128], jnp.concatenate(lows, axis=1), preferred_element_type=F32
            )
            total = high[:128] + high[128:] + low
            out = [total[:, :128], total[:, 128:]]
        return [block.reshape(8, LY, 128) for block in out]

    pairs = chebyshev_coefficients()

    def operator(updates):
        laps = laplace(updates)
        return [mass[...] * (lap + SIGMA_SHIFT * u) for lap, u in zip(laps, updates)]

    def source_parts(j):
        group = source_faces(j)
        for c in range(3):
            faces = group.field(c)

            def local(es, c=c):
                blocks = [basis[j + 1, c, planes(e)] for e in es]
                return [mass[...] * out for out in divergence(c, blocks)]

            def emit(e, w, c=c, faces=faces):
                parts[j, c, planes(e)] = w
                faces.rows(e, w)

            assembled(local, emit, faces.keep_ends)
        group.post_all()

    def krylov(j, last):
        now = lax.rem(j, 2)
        later = 1 - now
        for c in range(4):
            here = velocity_faces(now, c)
            there = velocity_faces(later, c)
            gate = here.corners_arrived if c == 0 and not last else None
            if gate is None:
                here.arrived()
            else:
                here.faces_arrived()
            totals = [jnp.zeros((8, 128), F32)] * 3
            if not last:

                @pl.when(j >= 1)
                def _(there=there):
                    there.sent()

            def local(es, c=c, totals=totals, here=here):
                blocks = []
                for e in es:
                    v = basis[j + 1, c, planes(e)] + free[planes(e)] * halo(
                        here.receive, here.corner_receive, e
                    )
                    basis[j + 1, c, planes(e)] = v
                    weighted = v * part[...]
                    totals[0] = totals[0] + tile_sum(weighted * v)
                    totals[1] = totals[1] + tile_sum(weighted * basis[j, c, planes(e)])
                    blocks.append(v)
                out = []
                for e, v, lap in zip(es, blocks, laplace(blocks)):
                    w = mass[...] * lap + minv[c // 3, planes(e)] * v
                    if last:
                        totals[2] = totals[2] + tile_sum(w * v)
                    out.append(w)
                return out

            def emit(e, w, c=c, there=there):
                basis[j + 2, c, planes(e)] = (
                    free[planes(e)] * w
                    - shift * basis[j + 1, c, planes(e)]
                    - basis[j, c, planes(e)]
                )
                there.rows(e, w)

            if last:
                for es in ((0, 3), (1, 2)):
                    local(es)
            else:
                assembled(local, emit, there.ends, there.done, gate)
            record(4 * j + c, totals[0])
            record(4 * (ITERS + j) + c, totals[1])
            if last:
                record(4 * 2 * ITERS + c, totals[2])

    def krylov_body(j, carry):
        krylov(j, False)

        source_parts(j)
        return carry

    lax.fori_loop(0, ITERS - 1, krylov_body, 0)
    krylov(jnp.int32(ITERS - 1), True)

    value = jnp.sum(macc[...], axis=0, keepdims=True)
    posted = []
    for k, partners in enumerate(stages):
        arow[k] = value
        copies = []
        for mask, device in partners:
            copy = pltpu.make_async_remote_copy(
                src_ref=arow.at[k],
                dst_ref=arcv.at[k, mask],
                send_sem=ass.at[k, mask],
                recv_sem=ars.at[k, mask],
                device_id=device,
                device_id_type=MESH,
            )
            copy.start()
            copies.append(copy)
        if k == 0:
            source_parts(jnp.int32(ITERS - 1))
        for (mask, _), copy in zip(partners, copies):
            copy.wait_recv()
        for mask, _ in partners:
            value = value + arcv[k, mask]
        posted.extend(copies)

    def moment(index):
        return value if index == 0 else pltpu.roll(value, 128 - 4 * index, 1)

    q = [moment(j) for j in range(ITERS)]
    r = [moment(ITERS + j) for j in range(1, ITERS)]
    r.append(moment(2 * ITERS) - shift * q[-1] - r[-1])
    nu = []
    for j in range(ITERS):
        nu.append(q[j] - q[j - 1] if j else q[0])
        nu.append(r[j] - r[j - 1] if j else r[0])

    def gram(i, j):
        total = None
        for k in range(min(i, j) + 1):
            term = nu[abs(i - j) + 2 * k]
            total = term if total is None else total + term
        return total

    system = [[None] * ITERS for _ in range(ITERS)]
    for i in range(ITERS):
        for j in range(i, ITERS):
            entry = shift * gram(i, j) + gram(i, j + 1)
            if j:
                entry = entry + gram(i, j - 1)
            system[i][j] = entry
    right = [nu[i] for i in range(ITERS)]
    inverse = []
    for k in range(ITERS):
        inverse.append(1.0 / system[k][k])
        for i in range(k + 1, ITERS):
            factor = system[k][i] * inverse[k]
            for j in range(i, ITERS):
                system[i][j] = system[i][j] - factor * system[k][j]
            right[i] = right[i] - factor * right[k]
    answer = [None] * ITERS
    for k in reversed(range(ITERS)):
        total = right[k]
        for j in range(k + 1, ITERS):
            total = total - system[k][j] * answer[j]
        answer[k] = total * inverse[k]

    lane_row = lax.broadcasted_iota(jnp.int32, (1, 128), 1)

    def coefficients(c):
        out = []
        for j in range(ITERS):
            one = jnp.sum(jnp.where(lane_row == c, answer[j], 0.0), axis=1, keepdims=True)
            if c == 3:
                one = one * (1.0 / THERMAL)
            out.append(jnp.broadcast_to(one, (8, 128)).reshape(1, 8, 128))
        return out

    def combine(c, weights):
        for x in range(0, LX, 8):
            for y in range(0, LY, 8):
                where = (pl.ds(x, 8), pl.ds(y, 8))
                total = weights[0] * basis[1, c, where[0], where[1]]
                for j in range(1, ITERS):
                    total = total + weights[j] * basis[j + 1, c, where[0], where[1]]
                fields[c, where[0], where[1]] = total

    known = [coefficients(c) for c in range(3)]
    for j in range(ITERS):
        source_faces(j).arrived()
    for r in range(0, FACE_ROWS, 8):
        total = None
        for c in range(3):
            for j in range(ITERS):
                term = known[c][j][0] * srcv[j, c, pl.ds(r, 8), :]
                total = term if total is None else total + term
        hsum[pl.ds(r, 8), :] = total
    for k in range(4):
        total = None
        for c in range(3):
            for j in range(ITERS):
                term = known[c][j][0, :1] * scrcv[j, c, k]
                total = term if total is None else total + term
        hcsum[k] = total

    for e in range(ELEMENTS):
        border = halo(hsum, hcsum, e)
        for x in range(8):
            for y in (0, 8):
                where = (8 * e + x, pl.ds(y, 8))
                total = border[x, y : y + 8]
                for c in range(3):
                    for j in range(ITERS):
                        total = total + known[c][j][0] * parts[j, c, where[0], where[1]]
                left = -free[where[0], where[1]] * total
                update = pairs[0][1] * (invd[x, pl.ds(y, 8)] * left)
                rem[where[0], where[1]] = left
                upd[where[0], where[1]] = update
                prs[where[0], where[1]] = update

    def apply_pressure(local, faces):
        def emit(e, w):
            rem[planes(e)] = rem[planes(e)] - free[planes(e)] * w
            faces.rows(e, w)

        assembled(local, emit, faces.ends, faces.done)

    apply_pressure(lambda es: operator([upd[planes(e)] for e in es]), pressure_faces(0))
    for c in range(3):
        combine(c, known[c])
    combine(3, coefficients(3))

    def refreshed(e, faces, keep, gain):
        left = rem[planes(e)] - free[planes(e)] * halo(faces.receive, faces.corner_receive, e)
        update = keep * upd[planes(e)] + gain * (invd[...] * left)
        prs[planes(e)] = prs[planes(e)] + update
        return left, update

    def chebyshev_body(i, carry):
        now = lax.rem(i + 1, 2)
        here = pressure_faces(now)
        there = pressure_faces(1 - now)
        keep, gain = jnp.float32(pairs[1][0]), jnp.float32(pairs[1][1])
        for k in range(2, CHEB - 1):
            keep = jnp.where(i == k, jnp.float32(pairs[k][0]), keep)
            gain = jnp.where(i == k, jnp.float32(pairs[k][1]), gain)

        here.arrived()

        @pl.when(i >= 2)
        def _():
            there.sent()

        def local(es):
            updates = []
            for e in es:
                left, update = refreshed(e, here, keep, gain)
                rem[planes(e)] = left
                upd[planes(e)] = update
                updates.append(update)
            return operator(updates)

        apply_pressure(local, there)
        return carry

    lax.fori_loop(1, CHEB - 1, chebyshev_body, 0)
    here = pressure_faces(CHEB % 2)
    here.arrived()
    for e in range(ELEMENTS):
        refreshed(e, here, pairs[CHEB - 1][0], pairs[CHEB - 1][1])
    for copy in posted:
        copy.wait_send()
    for slot in range(2):
        pressure_faces(slot).sent()
        for c in range(4):
            velocity_faces(slot, c).sent()
    for j in range(ITERS):
        source_faces(j).sent()


def store_kernel(fields, pressure, new_hbm, prs_hbm, sems):
    stores = [
        pltpu.make_async_copy(fields, new_hbm, sems.at[0]),
        pltpu.make_async_copy(pressure, prs_hbm, sems.at[1]),
    ]
    for store in stores:
        store.start()
    for store in stores:
        store.wait()


def solution(mesh):
    nx, ny = mesh.shape["gx"], mesh.shape["gy"]
    stages = reduction_stages(nx, ny)
    most = max(1 << len(bits) for bits in stages)
    matrices = matrix_tables()
    tables = field_tables()
    brick = (LX, LY, LZ)

    def body(*refs):
        step_kernel(nx, ny, *refs)

    def on_device(old_fields, inverse_step, boundary):
        any_space = pl.BlockSpec(memory_space=pl.ANY)
        operands = (old_fields, inverse_step, boundary, jnp.asarray(matrices), jnp.asarray(tables))
        operands = [pltpu.with_memory_space_constraint(x, pltpu.HBM) for x in operands]
        results = pl.pallas_call(
            body,
            out_shape=(pltpu.VMEM((4,) + brick, F32), pltpu.VMEM(brick, F32)),
            in_specs=[any_space] * 5,
            out_specs=(pl.BlockSpec(memory_space=pltpu.VMEM),) * 2,
            scratch_shapes=[
                pltpu.VMEM((4,) + brick, F32),
                pltpu.VMEM(brick, F32),
                pltpu.VMEM(brick, jnp.int32),
                pltpu.VMEM(matrices.shape, jnp.bfloat16),
                pltpu.VMEM(tables.shape, F32),
                pltpu.VMEM(brick, F32),
                pltpu.VMEM((2,) + brick, F32),
                pltpu.VMEM((ITERS + 1, 4) + brick, F32),
                pltpu.VMEM((ITERS, 3) + brick, F32),
                pltpu.VMEM(brick, F32),
                pltpu.VMEM(brick, F32),
                pltpu.VMEM((2, 4, FACE_ROWS, 128), F32),
                pltpu.VMEM((2, 4, FACE_ROWS, 128), F32),
                pltpu.VMEM((2, 4, 4, 1, 128), F32),
                pltpu.VMEM((2, 4, 4, 1, 128), F32),
                pltpu.VMEM((2, FACE_ROWS, 128), F32),
                pltpu.VMEM((2, FACE_ROWS, 128), F32),
                pltpu.VMEM((2, 4, 1, 128), F32),
                pltpu.VMEM((2, 4, 1, 128), F32),
                pltpu.VMEM((ITERS, 3, FACE_ROWS, 128), F32),
                pltpu.VMEM((ITERS, 3, FACE_ROWS, 128), F32),
                pltpu.VMEM((ITERS, 3, 4, 1, 128), F32),
                pltpu.VMEM((ITERS, 3, 4, 1, 128), F32),
                pltpu.VMEM((FACE_ROWS, 128), F32),
                pltpu.VMEM((4, 1, 128), F32),
                pltpu.VMEM((8, 128), F32),
                pltpu.VMEM((len(stages), 1, 128), F32),
                pltpu.VMEM((len(stages), most, 1, 128), F32),
                pltpu.SemaphoreType.DMA((5,)),
                pltpu.SemaphoreType.DMA((4, 2, 4)),
                pltpu.SemaphoreType.DMA((4, 2)),
                pltpu.SemaphoreType.DMA((4, ITERS)),
                pltpu.SemaphoreType.DMA((len(stages), most)),
                pltpu.SemaphoreType.DMA((len(stages), most)),
            ],
            compiler_params=pltpu.CompilerParams(
                collective_id=0, has_side_effects=True, vmem_limit_bytes=40 * 1024 * 1024
            ),
        )(*operands)
        results = [pltpu.with_memory_space_constraint(x, pltpu.VMEM) for x in results]
        return pl.pallas_call(
            store_kernel,
            out_shape=(
                jax.ShapeDtypeStruct((4,) + brick, F32),
                jax.ShapeDtypeStruct(brick, F32),
            ),
            in_specs=[any_space] * 2,
            out_specs=(any_space, any_space),
            scratch_shapes=[pltpu.SemaphoreType.DMA((2,))],
            compiler_params=pltpu.CompilerParams(vmem_limit_bytes=8 * 1024 * 1024),
        )(*results)

    return jax.shard_map(
        on_device,
        mesh=mesh,
        in_specs=(P(None, "gx", "gy", None), P("gx", "gy", None), P("gx", "gy", None)),
        out_specs=(P(None, "gx", "gy", None), P("gx", "gy", None)),
        check_vma=False,
    )
```

```python
import jax
import jax.numpy as jnp
import ml_dtypes
import numpy as np
from jax import lax
from jax.experimental import pallas as pl
from jax.experimental.pallas import tpu as pltpu
from jax.sharding import PartitionSpec as P

ITERS = 6
CHEB = 6
SIGMA_SHIFT = 0.5
THERMAL = 1.4
COUPLING = 1.0
STRATIFY = 1.0
SPREAD = 20.0
CENTRE = 6.0
HALF = 2.9
LOBATTO_POINTS = (
    -1.0,
    -0.8717401485096066,
    -0.5917001814331423,
    -0.2092992179024789,
    0.2092992179024789,
    0.5917001814331423,
    0.8717401485096066,
    1.0,
)
MESH = pl.DeviceIdType.MESH
LX, LY, LZ = 32, 16, 128
ELEMENTS = LX // 8
F32 = jnp.float32
X_FACES = ((-1, 0, 0, 16, 16), (1, 0, 16, 0, 16))
Y_FACES = ((0, -1, 32, 64, 32), (0, 1, 64, 32, 32))
FACE_ROWS = 96
CORNERS = ((-1, -1, 0, 3), (-1, 1, 1, 2), (1, -1, 2, 1), (1, 1, 3, 0))


def legendre_value(points, degree):
    previous = points * 0.0 + 1.0
    current = points
    for order in range(1, degree):
        following = ((2 * order + 1) * points * current - order * previous) / (order + 1)
        previous = current
        current = following
    return current


def quadrature_tables():
    degree = 7
    points = np.array(LOBATTO_POINTS)
    values = legendre_value(points, degree)
    weights = 2.0 / (degree * (degree + 1) * values * values)
    derive = np.zeros((degree + 1, degree + 1))
    for row in range(degree + 1):
        for column in range(degree + 1):
            if row != column:
                derive[row, column] = values[row] / (
                    values[column] * (points[row] - points[column])
                )
    derive[0, 0] = -degree * (degree + 1) / 4.0
    derive[degree, degree] = degree * (degree + 1) / 4.0
    return weights, derive, derive.T @ (weights[:, None] * derive)


def chebyshev_bounds():
    weights, _, stiff = quadrature_tables()
    w = np.diag(weights)
    element = np.kron(np.kron(stiff, w), w)
    element = element + np.kron(np.kron(w, stiff), w)
    element = element + np.kron(np.kron(w, w), stiff)
    element = element + SIGMA_SHIFT * np.kron(np.kron(w, w), w)
    upper = float(np.max(np.sum(np.abs(element), axis=1) / np.diag(element)))
    lower = upper / SPREAD
    return (upper + lower) / 2.0, (upper - lower) / 2.0


def chebyshev_coefficients():
    centre, half = chebyshev_bounds()
    ratio = centre / half
    damping = 1.0 / ratio
    pairs = [(0.0, 1.0 / centre)]
    for _ in range(CHEB - 1):
        following = 1.0 / (2.0 * ratio - damping)
        pairs.append((following * damping, 2.0 * following / half))
        damping = following
    return pairs


def split_pair(matrix):
    high = matrix.astype(ml_dtypes.bfloat16)
    low = (matrix - high.astype(np.float64)).astype(ml_dtypes.bfloat16)
    return high, low


def left_table(matrix):
    high, low = split_pair(matrix)
    return np.block([[high, high], [low, np.zeros_like(low)]])


def right_table(matrix):
    high, low = split_pair(matrix)
    return np.block([[high, low], [high, np.zeros_like(low)]])


def matrix_tables():
    weights, derive, stiff = quadrature_tables()
    scaled = stiff / weights[:, None]
    eye_y = np.eye(LY // 8)
    eye_z = np.eye(LZ // 8)
    lap_xy = np.kron(scaled, np.eye(LY)) + np.kron(np.eye(8), np.kron(eye_y, scaled))
    lap_z = np.kron(eye_z, scaled).T
    div_xy = np.concatenate(
        [np.kron(derive, np.eye(LY)), np.kron(np.eye(8), np.kron(eye_y, derive))], axis=1
    )
    div_z = np.kron(eye_z, derive).T
    return np.stack(
        [
            left_table(lap_xy),
            right_table(lap_z),
            np.concatenate(split_pair(div_xy), axis=0),
            right_table(div_z),
        ]
    )


def field_tables():
    weights, _, stiff = quadrature_tables()
    mass = weights[:, None, None] * np.tile(weights, 2)[None, :, None] * np.tile(weights, 16)
    shared = np.where(np.arange(8) % 7 == 0, 0.5, 1.0)
    shared_z = np.tile(shared, 16)
    shared_z[0] = shared_z[-1] = 1.0
    part = shared[:, None, None] * np.tile(shared, 2)[None, :, None] * shared_z

    def periodic(line):
        line = line.copy()
        line[0] = line[7] = line[0] + line[7]
        return line

    def column(line):
        line = np.tile(line, 16)
        total = line.copy()
        total[8::8] += line[7:-1:8]
        total[7:-1:8] += line[8::8]
        return total

    entry = np.diag(stiff)
    wx, sx = periodic(weights), periodic(entry)
    wy, sy = np.tile(wx, 2), np.tile(sx, 2)
    wz, sz = column(weights), column(entry)

    def outer(a, b, c):
        return a[:, None, None] * b[None, :, None] * c

    diagonal = outer(sx, wy, wz) + outer(wx, sy, wz) + outer(wx, wy, sz)
    diagonal = diagonal + SIGMA_SHIFT * outer(wx, wy, wz)
    return np.stack([mass / HALF, part, HALF / diagonal]).astype(np.float32)


def reduction_stages(nx, ny):
    bits_y = ny.bit_length() - 1
    bits = list(range(bits_y + nx.bit_length() - 1))
    first = [b for b in bits if b == 1 or b >= bits_y]
    stages = [first, [b for b in bits if b not in first]]
    return [stage for stage in stages if stage]


def step_kernel(nx, ny, *refs):
    (old_hbm, inv_hbm, bnd_hbm, mat_hbm, tab_hbm, fields, prs) = refs[:7]
    (old, inv, bnd, mat_ref, tab_ref, free, minv, basis, parts, rem, upd) = refs[7:18]
    (vsnd, vrcv, vcsnd, vcrcv, psnd, prcv, pcsnd, pcrcv) = refs[18:26]
    (ssnd, srcv, scsnd, scrcv, hsum, hcsum, macc, arow, arcv) = refs[26:35]
    (lsem, vsem, psem, ssem, ass, ars) = refs[35:]

    gx = lax.axis_index("gx")
    gy = lax.axis_index("gy")

    def neighbour(dx, dy):
        return (lax.rem(gx + dx + nx, nx), lax.rem(gy + dy + ny, ny))

    me = gx * ny + gy
    bits_y = ny.bit_length() - 1

    def hops(b):
        if b < 2:
            return 2 * b
        return 1 << (b - 2) if b < bits_y else max(1, b - bits_y)

    stages = []
    for bits in reduction_stages(nx, ny):
        partners = []
        masks = range(1, 1 << len(bits))
        masks = sorted(masks, key=lambda m: -sum(hops(b) for i, b in enumerate(bits) if m >> i & 1))
        for mask in masks:
            other = me
            for place, b in enumerate(bits):
                if mask >> place & 1:
                    other = other + (1 - 2 * lax.rem(lax.div(me, 1 << b), 2)) * (1 << b)
            partners.append((mask, (lax.div(other, ny), lax.rem(other, ny))))
        stages.append(partners)

    barrier = pltpu.get_barrier_semaphore()
    greeted = 0
    for dx, dy, *_ in CORNERS + Y_FACES + X_FACES:
        pl.semaphore_signal(barrier, inc=1, device_id=neighbour(dx, dy), device_id_type=MESH)
        greeted += 1
    for partners in stages:
        for _, device in partners:
            pl.semaphore_signal(barrier, inc=1, device_id=device, device_id_type=MESH)
            greeted += 1

    loads = [
        pltpu.make_async_copy(inv_hbm, inv, lsem.at[0]),
        pltpu.make_async_copy(bnd_hbm, bnd, lsem.at[1]),
        pltpu.make_async_copy(tab_hbm, tab_ref, lsem.at[2]),
        pltpu.make_async_copy(old_hbm, old, lsem.at[3]),
        pltpu.make_async_copy(mat_hbm, mat_ref, lsem.at[4]),
    ]
    for load in loads:
        load.start()

    lane = lax.broadcasted_iota(jnp.int32, (128, 128), 1)
    z_first = (lax.rem(lane, 8) == 0) & (lane > 0)
    z_last = (lax.rem(lane, 8) == 7) & (lane < LZ - 1)
    row3 = lax.broadcasted_iota(jnp.int32, (8, 8, 128), 1)
    row3_first, row3_last = row3 == 0, row3 == 7
    row = lax.broadcasted_iota(jnp.int32, (8, 128), 0)
    row_first, row_last = row == 0, row == 7
    tile_lane = lax.broadcasted_iota(jnp.int32, (8, 128), 1)

    def planes(e):
        return pl.ds(8 * e, 8)

    def inner_sums(w):
        flat = w.reshape(128, 128)
        flat = (
            flat
            + jnp.where(z_first, pltpu.roll(flat, 1, 1), 0.0)
            + jnp.where(z_last, pltpu.roll(flat, 127, 1), 0.0)
        )
        w = flat.reshape(8, LY, 128)
        a, b = w[:, :8], w[:, 8:]
        a_sum = a + jnp.where(row3_last, pltpu.roll(b, 7, 1), 0.0)
        b_sum = b + jnp.where(row3_first, pltpu.roll(a, 1, 1), 0.0)
        return jnp.concatenate([a_sum, b_sum], axis=1)

    def assembled(local, emit, ends=None, done=None, gate=None):
        if gate is not None:
            w1, w2 = [inner_sums(w) for w in local((1, 2))]
            gate()
        w0, w3 = [inner_sums(w) for w in local((0, 3))]
        if ends is not None:
            ends(w0, w3)
        if gate is None:
            w1, w2 = [inner_sums(w) for w in local((1, 2))]
        both = w0[7:] + w1[:1]
        emit(0, jnp.concatenate([w0[:7], both], axis=0))
        w1 = jnp.concatenate([both, w1[1:]], axis=0)
        both = w1[7:] + w2[:1]
        emit(1, jnp.concatenate([w1[:7], both], axis=0))
        w2 = jnp.concatenate([both, w2[1:]], axis=0)
        both = w2[7:] + w3[:1]
        emit(2, jnp.concatenate([w2[:7], both], axis=0))
        emit(3, jnp.concatenate([both, w3[1:]], axis=0))
        if done is not None:
            done()

    class Faces:
        def __init__(self, send, receive, corner_send, corner_receive, sems):
            self.send, self.receive = send, receive
            self.corner_send, self.corner_receive = corner_send, corner_receive
            self.sems = sems

        def start(self, source, target, dx, dy, k):
            pltpu.make_async_remote_copy(
                src_ref=source,
                dst_ref=target,
                send_sem=self.sems(k),
                recv_sem=self.sems(k + 1),
                device_id=neighbour(dx, dy),
                device_id_type=MESH,
            ).start()

        def post(self, faces):
            for dx, dy, here, there, rows in faces:
                here, there = pl.ds(here, rows), pl.ds(there, rows)
                if len(self.send.shape) == 3:
                    source, target = self.send.at[:, here], self.receive.at[:, there]
                else:
                    source, target = self.send.at[here], self.receive.at[there]
                self.start(source, target, dx, dy, 0)

        def post_corners(self):
            for dx, dy, here, there in CORNERS:
                if len(self.send.shape) == 3:
                    source, target = self.corner_send.at[:, here], self.corner_receive.at[:, there]
                else:
                    source, target = self.corner_send.at[here], self.corner_receive.at[there]
                self.start(source, target, dx, dy, 2)

        def field(self, c):
            return Faces(
                self.send.at[c],
                self.receive.at[c],
                self.corner_send.at[c],
                self.corner_receive.at[c],
                self.sems,
            )

        def keep_corners(self, w0, w3):
            self.corner_send[0] = w0[0, :1]
            self.corner_send[1] = w0[0, LY - 1 :]
            self.corner_send[2] = w3[7, :1]
            self.corner_send[3] = w3[7, LY - 1 :]

        def keep_sides(self, w0, w3):
            self.send[pl.ds(0, 16), :] = w0[0]
            self.send[pl.ds(16, 16), :] = w3[7]

        def keep_ends(self, w0, w3):
            self.keep_corners(w0, w3)
            self.keep_sides(w0, w3)

        def ends(self, w0, w3):
            self.keep_corners(w0, w3)
            self.post_corners()
            self.keep_sides(w0, w3)
            self.post(X_FACES)

        def rows(self, e, w):
            self.send[pl.ds(32 + 8 * e, 8), :] = w[:, 0, :]
            self.send[pl.ds(64 + 8 * e, 8), :] = w[:, LY - 1, :]

        def done(self):
            self.post(Y_FACES)

        def post_all(self):
            self.post_corners()
            self.post(Y_FACES + X_FACES)

        def arrived(self):
            wait_all(self.receive, self.sems(1))
            wait_all(self.corner_receive, self.sems(3))

        def faces_arrived(self):
            wait_all(self.receive, self.sems(1))

        def corners_arrived(self):
            wait_all(self.corner_receive, self.sems(3))

        def sent(self):
            wait_all(self.send, self.sems(0))
            wait_all(self.corner_send, self.sems(2))

    def velocity_faces(slot, c):
        return Faces(
            vsnd.at[slot, c],
            vrcv.at[slot, c],
            vcsnd.at[slot, c],
            vcrcv.at[slot, c],
            lambda k: vsem.at[k, slot, c],
        )

    def pressure_faces(slot):
        return Faces(
            psnd.at[slot],
            prcv.at[slot],
            pcsnd.at[slot],
            pcrcv.at[slot],
            lambda k: psem.at[k, slot],
        )

    def source_faces(j):
        return Faces(
            ssnd.at[j], srcv.at[j], scsnd.at[j], scrcv.at[j], lambda k: ssem.at[k, j]
        )

    def spread_row(line):
        return jnp.broadcast_to(line, (8, 128))

    def halo(faces, corners, e):
        out = []
        for x in range(8):
            first = spread_row(faces[pl.ds(32 + 8 * e + x, 1), :])
            last = spread_row(faces[pl.ds(64 + 8 * e + x, 1), :])
            side = None
            if e == 0 and x == 0:
                side, corner = 0, 0
            if e == ELEMENTS - 1 and x == 7:
                side, corner = 16, 2
            if side is not None:
                first = first + spread_row(corners[corner])
                last = last + spread_row(corners[corner + 1])
            first = jnp.where(row_first, first, 0.0)
            last = jnp.where(row_last, last, 0.0)
            if side is not None:
                first = first + faces[pl.ds(side, 8), :]
                last = last + faces[pl.ds(side + 8, 8), :]
            out.append(jnp.concatenate([first, last], axis=0))
        return jnp.stack(out)

    def wait_all(ref, sem):
        pltpu.make_async_copy(ref, ref, sem).wait()

    def halves(v):
        high = v.astype(jnp.bfloat16)
        return high, (v - high.astype(F32)).astype(jnp.bfloat16)

    def along_z(highs, lows, index):
        rows = [jnp.concatenate([h, l], axis=1) for h, l in zip(highs, lows)]
        out = jnp.dot(
            jnp.concatenate(rows, axis=0), mat_ref[index], preferred_element_type=F32
        )
        out = out[:, :128] + out[:, 128:]
        return [out[:128], out[128:]]

    def split_blocks(blocks):
        pairs = [halves(v.reshape(128, 128)) for v in blocks]
        return [p[0] for p in pairs], [p[1] for p in pairs]

    def laplace(blocks):
        highs, lows = split_blocks(blocks)
        stacked = jnp.concatenate(
            [jnp.concatenate(highs, axis=1), jnp.concatenate(lows, axis=1)], axis=0
        )
        xy = jnp.dot(mat_ref[0], stacked, preferred_element_type=F32)
        xy = xy[:128] + xy[128:]
        z = along_z(highs, lows, 1)
        return [
            (xy[:, :128] + z[0]).reshape(8, LY, 128),
            (xy[:, 128:] + z[1]).reshape(8, LY, 128),
        ]

    mass, part, invd = tab_ref.at[0], tab_ref.at[1], tab_ref.at[2]

    def tile_sum(a):
        a = a.reshape(16, 8, 128)
        total = a[0]
        for k in range(1, 16):
            total = total + a[k]
        return total

    def record(slot, total):
        lanes = jnp.sum(total, axis=1, keepdims=True)
        macc[...] += jnp.where(tile_lane == slot, lanes, 0.0)

    for load in loads[:3]:
        load.wait()
    macc[...] = jnp.zeros_like(macc)
    for e in range(ELEMENTS):
        free[planes(e)] = bnd[planes(e)].astype(F32)
        scaled = mass[...] * inv[planes(e)]
        minv[0, planes(e)] = scaled
        minv[1, planes(e)] = scaled * (1.0 / THERMAL)
        for c in range(4):
            basis[0, c, planes(e)] = jnp.zeros((8, LY, 128), F32)
    loads[3].wait()

    for c in range(4):

        def local_right(e, c=c):
            value = minv[0, planes(e)] * old[c, planes(e)]
            if c == 2:
                value = value + mass[...] * (COUPLING * old[3, planes(e)])
            if c == 3:
                value = value - mass[...] * (STRATIFY * old[2, planes(e)])
            return value

        faces = velocity_faces(0, c)

        def emit_right(e, w, c=c, faces=faces):
            basis[1, c, planes(e)] = free[planes(e)] * w
            faces.rows(e, w)

        def ends_right(w0, w3, c=c, faces=faces):
            if c == 0:
                pl.semaphore_wait(barrier, greeted)
            faces.ends(w0, w3)

        assembled(lambda es, f=local_right: [f(e) for e in es], emit_right, ends_right, faces.done)
    loads[4].wait()

    shift = CENTRE / HALF

    def divergence(c, blocks):
        highs, lows = split_blocks(blocks)
        if c == 2:
            out = along_z(highs, lows, 3)
        else:
            table = mat_ref[2, :, pl.ds(128 * c, 128)]
            high = jnp.dot(table, jnp.concatenate(highs, axis=1), preferred_element_type=F32)
            low = jnp.dot(
                table[:128], jnp.concatenate(lows, axis=1), preferred_element_type=F32
            )
            total = high[:128] + high[128:] + low
            out = [total[:, :128], total[:, 128:]]
        return [block.reshape(8, LY, 128) for block in out]

    pairs = chebyshev_coefficients()

    def operator(updates):
        laps = laplace(updates)
        return [mass[...] * (lap + SIGMA_SHIFT * u) for lap, u in zip(laps, updates)]

    def source_parts(j):
        group = source_faces(j)
        for c in range(3):
            faces = group.field(c)

            def local(es, c=c):
                blocks = [basis[j + 1, c, planes(e)] for e in es]
                return [mass[...] * out for out in divergence(c, blocks)]

            def emit(e, w, c=c, faces=faces):
                parts[j, c, planes(e)] = w
                faces.rows(e, w)

            assembled(local, emit, faces.keep_ends)
        group.post_all()

    def krylov(j, last):
        now = lax.rem(j, 2)
        later = 1 - now
        for c in range(4):
            here = velocity_faces(now, c)
            there = velocity_faces(later, c)
            gate = here.corners_arrived if c == 0 and not last else None
            if gate is None:
                here.arrived()
            else:
                here.faces_arrived()
            totals = [jnp.zeros((8, 128), F32)] * 3
            if not last:

                @pl.when(j >= 1)
                def _(there=there):
                    there.sent()

            def local(es, c=c, totals=totals, here=here):
                blocks = []
                for e in es:
                    v = basis[j + 1, c, planes(e)] + free[planes(e)] * halo(
                        here.receive, here.corner_receive, e
                    )
                    basis[j + 1, c, planes(e)] = v
                    weighted = v * part[...]
                    totals[0] = totals[0] + tile_sum(weighted * v)
                    totals[1] = totals[1] + tile_sum(weighted * basis[j, c, planes(e)])
                    blocks.append(v)
                out = []
                for e, v, lap in zip(es, blocks, laplace(blocks)):
                    w = mass[...] * lap + minv[c // 3, planes(e)] * v
                    if last:
                        totals[2] = totals[2] + tile_sum(w * v)
                    out.append(w)
                return out

            def emit(e, w, c=c, there=there):
                basis[j + 2, c, planes(e)] = (
                    free[planes(e)] * w
                    - shift * basis[j + 1, c, planes(e)]
                    - basis[j, c, planes(e)]
                )
                there.rows(e, w)

            if last:
                for es in ((0, 3), (1, 2)):
                    local(es)
            else:
                assembled(local, emit, there.ends, there.done, gate)
            record(4 * j + c, totals[0])
            record(4 * (ITERS + j) + c, totals[1])
            if last:
                record(4 * 2 * ITERS + c, totals[2])

    def krylov_body(j, carry):
        krylov(j, False)

        source_parts(j)
        return carry

    lax.fori_loop(0, ITERS - 1, krylov_body, 0)
    krylov(jnp.int32(ITERS - 1), True)

    value = jnp.sum(macc[...], axis=0, keepdims=True)
    posted = []
    for k, partners in enumerate(stages):
        arow[k] = value
        copies = []
        for mask, device in partners:
            copy = pltpu.make_async_remote_copy(
                src_ref=arow.at[k],
                dst_ref=arcv.at[k, mask],
                send_sem=ass.at[k, mask],
                recv_sem=ars.at[k, mask],
                device_id=device,
                device_id_type=MESH,
            )
            copy.start()
            copies.append(copy)
        if k == 0:
            source_parts(jnp.int32(ITERS - 1))
        for (mask, _), copy in zip(partners, copies):
            copy.wait_recv()
        for mask, _ in partners:
            value = value + arcv[k, mask]
        posted.extend(copies)

    def moment(index):
        return value if index == 0 else pltpu.roll(value, 128 - 4 * index, 1)

    q = [moment(j) for j in range(ITERS)]
    r = [moment(ITERS + j) for j in range(1, ITERS)]
    r.append(moment(2 * ITERS) - shift * q[-1] - r[-1])
    nu = []
    for j in range(ITERS):
        nu.append(q[j] - q[j - 1] if j else q[0])
        nu.append(r[j] - r[j - 1] if j else r[0])

    def gram(i, j):
        total = None
        for k in range(min(i, j) + 1):
            term = nu[abs(i - j) + 2 * k]
            total = term if total is None else total + term
        return total

    system = [[None] * ITERS for _ in range(ITERS)]
    for i in range(ITERS):
        for j in range(i, ITERS):
            entry = shift * gram(i, j) + gram(i, j + 1)
            if j:
                entry = entry + gram(i, j - 1)
            system[i][j] = entry
    right = [nu[i] for i in range(ITERS)]
    inverse = []
    for k in range(ITERS):
        inverse.append(1.0 / system[k][k])
        for i in range(k + 1, ITERS):
            factor = system[k][i] * inverse[k]
            for j in range(i, ITERS):
                system[i][j] = system[i][j] - factor * system[k][j]
            right[i] = right[i] - factor * right[k]
    answer = [None] * ITERS
    for k in reversed(range(ITERS)):
        total = right[k]
        for j in range(k + 1, ITERS):
            total = total - system[k][j] * answer[j]
        answer[k] = total * inverse[k]

    lane_row = lax.broadcasted_iota(jnp.int32, (1, 128), 1)

    def coefficients(c):
        out = []
        for j in range(ITERS):
            one = jnp.sum(jnp.where(lane_row == c, answer[j], 0.0), axis=1, keepdims=True)
            if c == 3:
                one = one * (1.0 / THERMAL)
            out.append(jnp.broadcast_to(one, (8, 128)).reshape(1, 8, 128))
        return out

    def combine(c, weights):
        for x in range(0, LX, 8):
            for y in range(0, LY, 8):
                where = (pl.ds(x, 8), pl.ds(y, 8))
                total = weights[0] * basis[1, c, where[0], where[1]]
                for j in range(1, ITERS):
                    total = total + weights[j] * basis[j + 1, c, where[0], where[1]]
                fields[c, where[0], where[1]] = total

    known = [coefficients(c) for c in range(3)]
    for j in range(ITERS):
        source_faces(j).arrived()
    for r in range(0, FACE_ROWS, 8):
        total = None
        for c in range(3):
            for j in range(ITERS):
                term = known[c][j][0] * srcv[j, c, pl.ds(r, 8), :]
                total = term if total is None else total + term
        hsum[pl.ds(r, 8), :] = total
    for k in range(4):
        total = None
        for c in range(3):
            for j in range(ITERS):
                term = known[c][j][0, :1] * scrcv[j, c, k]
                total = term if total is None else total + term
        hcsum[k] = total

    for e in range(ELEMENTS):
        border = halo(hsum, hcsum, e)
        for x in range(8):
            for y in (0, 8):
                where = (8 * e + x, pl.ds(y, 8))
                total = border[x, y : y + 8]
                for c in range(3):
                    for j in range(ITERS):
                        total = total + known[c][j][0] * parts[j, c, where[0], where[1]]
                left = -free[where[0], where[1]] * total
                update = pairs[0][1] * (invd[x, pl.ds(y, 8)] * left)
                rem[where[0], where[1]] = left
                upd[where[0], where[1]] = update
                prs[where[0], where[1]] = update

    def apply_pressure(local, faces):
        def emit(e, w):
            rem[planes(e)] = rem[planes(e)] - free[planes(e)] * w
            faces.rows(e, w)

        assembled(local, emit, faces.ends, faces.done)

    apply_pressure(lambda es: operator([upd[planes(e)] for e in es]), pressure_faces(0))
    for c in range(3):
        combine(c, known[c])
    combine(3, coefficients(3))

    def refreshed(e, faces, keep, gain):
        left = rem[planes(e)] - free[planes(e)] * halo(faces.receive, faces.corner_receive, e)
        update = keep * upd[planes(e)] + gain * (invd[...] * left)
        prs[planes(e)] = prs[planes(e)] + update
        return left, update

    def chebyshev_body(i, carry):
        now = lax.rem(i + 1, 2)
        here = pressure_faces(now)
        there = pressure_faces(1 - now)
        keep, gain = jnp.float32(pairs[1][0]), jnp.float32(pairs[1][1])
        for k in range(2, CHEB - 1):
            keep = jnp.where(i == k, jnp.float32(pairs[k][0]), keep)
            gain = jnp.where(i == k, jnp.float32(pairs[k][1]), gain)

        here.arrived()

        @pl.when(i >= 2)
        def _():
            there.sent()

        def local(es):
            updates = []
            for e in es:
                left, update = refreshed(e, here, keep, gain)
                rem[planes(e)] = left
                upd[planes(e)] = update
                updates.append(update)
            return operator(updates)

        apply_pressure(local, there)
        return carry

    lax.fori_loop(1, CHEB - 1, chebyshev_body, 0)
    for copy in posted:
        copy.wait_send()
    for slot in range(2):
        for c in range(4):
            velocity_faces(slot, c).sent()
    for j in range(ITERS):
        source_faces(j).sent()
    pressure_faces(CHEB % 2 + 1).sent()
    here = pressure_faces(CHEB % 2)
    here.sent()
    here.faces_arrived()
    for e in (1, 2):
        refreshed(e, here, pairs[CHEB - 1][0], pairs[CHEB - 1][1])
    here.corners_arrived()
    for e in (0, 3):
        refreshed(e, here, pairs[CHEB - 1][0], pairs[CHEB - 1][1])


def store_kernel(fields, pressure, new_hbm, prs_hbm, sems):
    stores = [
        pltpu.make_async_copy(fields, new_hbm, sems.at[0]),
        pltpu.make_async_copy(pressure, prs_hbm, sems.at[1]),
    ]
    for store in stores:
        store.start()
    for store in stores:
        store.wait()


def solution(mesh):
    nx, ny = mesh.shape["gx"], mesh.shape["gy"]
    stages = reduction_stages(nx, ny)
    most = max(1 << len(bits) for bits in stages)
    matrices = matrix_tables()
    tables = field_tables()
    brick = (LX, LY, LZ)

    def body(*refs):
        step_kernel(nx, ny, *refs)

    def on_device(old_fields, inverse_step, boundary):
        any_space = pl.BlockSpec(memory_space=pl.ANY)
        operands = (old_fields, inverse_step, boundary, jnp.asarray(matrices), jnp.asarray(tables))
        operands = [pltpu.with_memory_space_constraint(x, pltpu.HBM) for x in operands]
        results = pl.pallas_call(
            body,
            out_shape=(pltpu.VMEM((4,) + brick, F32), pltpu.VMEM(brick, F32)),
            in_specs=[any_space] * 5,
            out_specs=(pl.BlockSpec(memory_space=pltpu.VMEM),) * 2,
            scratch_shapes=[
                pltpu.VMEM((4,) + brick, F32),
                pltpu.VMEM(brick, F32),
                pltpu.VMEM(brick, jnp.int32),
                pltpu.VMEM(matrices.shape, jnp.bfloat16),
                pltpu.VMEM(tables.shape, F32),
                pltpu.VMEM(brick, F32),
                pltpu.VMEM((2,) + brick, F32),
                pltpu.VMEM((ITERS + 1, 4) + brick, F32),
                pltpu.VMEM((ITERS, 3) + brick, F32),
                pltpu.VMEM(brick, F32),
                pltpu.VMEM(brick, F32),
                pltpu.VMEM((2, 4, FACE_ROWS, 128), F32),
                pltpu.VMEM((2, 4, FACE_ROWS, 128), F32),
                pltpu.VMEM((2, 4, 4, 1, 128), F32),
                pltpu.VMEM((2, 4, 4, 1, 128), F32),
                pltpu.VMEM((2, FACE_ROWS, 128), F32),
                pltpu.VMEM((2, FACE_ROWS, 128), F32),
                pltpu.VMEM((2, 4, 1, 128), F32),
                pltpu.VMEM((2, 4, 1, 128), F32),
                pltpu.VMEM((ITERS, 3, FACE_ROWS, 128), F32),
                pltpu.VMEM((ITERS, 3, FACE_ROWS, 128), F32),
                pltpu.VMEM((ITERS, 3, 4, 1, 128), F32),
                pltpu.VMEM((ITERS, 3, 4, 1, 128), F32),
                pltpu.VMEM((FACE_ROWS, 128), F32),
                pltpu.VMEM((4, 1, 128), F32),
                pltpu.VMEM((8, 128), F32),
                pltpu.VMEM((len(stages), 1, 128), F32),
                pltpu.VMEM((len(stages), most, 1, 128), F32),
                pltpu.SemaphoreType.DMA((5,)),
                pltpu.SemaphoreType.DMA((4, 2, 4)),
                pltpu.SemaphoreType.DMA((4, 2)),
                pltpu.SemaphoreType.DMA((4, ITERS)),
                pltpu.SemaphoreType.DMA((len(stages), most)),
                pltpu.SemaphoreType.DMA((len(stages), most)),
            ],
            compiler_params=pltpu.CompilerParams(
                collective_id=0, has_side_effects=True, vmem_limit_bytes=40 * 1024 * 1024
            ),
        )(*operands)
        results = [pltpu.with_memory_space_constraint(x, pltpu.VMEM) for x in results]
        return pl.pallas_call(
            store_kernel,
            out_shape=(
                jax.ShapeDtypeStruct((4,) + brick, F32),
                jax.ShapeDtypeStruct(brick, F32),
            ),
            in_specs=[any_space] * 2,
            out_specs=(any_space, any_space),
            scratch_shapes=[pltpu.SemaphoreType.DMA((2,))],
            compiler_params=pltpu.CompilerParams(vmem_limit_bytes=8 * 1024 * 1024),
        )(*results)

    return jax.shard_map(
        on_device,
        mesh=mesh,
        in_specs=(P(None, "gx", "gy", None), P("gx", "gy", None), P("gx", "gy", None)),
        out_specs=(P(None, "gx", "gy", None), P("gx", "gy", None)),
        check_vma=False,
    )
```
